512 devices in a mesh: blk: 128 (over y, z, core), dp: 4 (over x).
Axes of the slice: x: 4, y: 8, z: 8, core: 2. Of those that a mesh axis runs over, the one named last changes fastest.
Arguments:
- hidden: bfloat16 [512, 32768], P('dp', 'blk'), may hold values from -6 to 6
- weights: bfloat16 [256, 26, 128, 256], P('blk'), may hold values from -0.109375 to 0.109375
- pattern: int32 [256, 26], replicated, may hold values from 0 to 255, as said below
- row_of_slot: int32 [256], replicated, may hold values from 0 to 255, as said below
- cotangent: bfloat16 [512, 32768], P('dp', 'blk'), may hold values from -6 to 6
Outputs:
- output: bfloat16 [512, 32768], P('dp', 'blk')
- input_grad: bfloat16 [512, 32768], P('dp', 'blk')
- weight_grad: bfloat16 [256, 26, 128, 256], P('blk', None, 'dp')
The draws below stay inside these ranges and needn't reach their ends.
Inputs may be any that keep to these rules, and one draw needn't show every extreme that they name: `row_of_slot`: A permutation of the block indices. `pattern`: the 26 entries of a row differ. The 52 slots source[p, k] read by the rows of one device lie on 52 different devices (slot q lies on device q // 2), so a device reads exactly one block from each device it reads from.
All inputs are finite; a program needn't handle non-finite values.
Results may differ from the reference program's by a relative error of at most 0.017.
Values may be sent and summed in bfloat16 or wider, within the bound.
No kernel may reach another device: no remote copies, remote signals or barrier semaphores. Data moves between devices by JAX's collectives and lax.ppermute only.
A program may use at most 64 MiB of HBM per device.

```python
import jax
import jax.numpy as jnp
from jax import lax

BS = 128
BPD = 2
TOK = 128
NB = 256
FF = 32768
K = 26
TOKENS = 512


def shared_pattern(key):
    devices = NB // BPD
    reads = BPD * K
    order = jax.random.permutation(jax.random.fold_in(key, 11), NB).astype(jnp.int32)
    popular = jax.random.randint(jax.random.fold_in(key, 12), (devices,), 1, 17)
    noise = jax.random.randint(jax.random.fold_in(key, 13), (devices, devices), 0, 4096)
    scores = noise * popular[None, :] * devices + jnp.arange(devices, dtype=jnp.int32)[None, :]
    unused, chosen = lax.top_k(scores, reads)
    which = jax.random.randint(jax.random.fold_in(key, 14), (devices, reads), 0, BPD)
    slots = chosen.astype(jnp.int32) * BPD + which
    columns = order[slots].reshape(NB, K).astype(jnp.int32)
    return (order, columns)


def draw_row_of_slot(key, part):
    parts = shared_pattern(key)
    return parts[0]


def draw_pattern(key, part):
    parts = shared_pattern(key)
    return parts[1]


def block_scale(stream_key, dims, split, least, top_value):
    gain, own = 1.0, jax.random.fold_in(stream_key, 6)
    for position, blocks in split:
        steps = jnp.exp(jax.random.uniform(jax.random.fold_in(own, position), (blocks,), jnp.float32, least / len(split), top_value / len(split)))
        gain = gain * jnp.repeat(steps, dims[position] // blocks).reshape([-1 if axis == position else 1 for axis in range(len(dims))])
    return gain


def scatter_about(stream_key, dims, deviation, bound, split=(), held_as=jnp.bfloat16):
    level = block_scale(stream_key, dims, split, -0.22, 0.18) if split else 1.0
    values = jax.random.normal(stream_key, dims, jnp.float32) * deviation * level
    return jnp.minimum(jnp.maximum(values, -bound), bound).astype(held_as)


def setup_inputs(seed: int = 0) -> dict:
    streams_of = jax.random.split(jax.random.key(seed), 6)
    hidden = scatter_about(streams_of[0], (TOKENS, FF), 1.0, 6.0, ((0, 4), (1, 128)))
    weights = scatter_about(streams_of[1], (NB, K, BS, 2 * BS), (K * BS) ** -0.5, 0.109375, ((0, 128),))
    pattern = draw_pattern(jax.random.fold_in(streams_of[5], 71), 0)
    row_of_slot = draw_row_of_slot(jax.random.fold_in(streams_of[5], 71), 0)
    cotangent = scatter_about(streams_of[4], (TOKENS, FF), 1.0, 6.0, ((0, 4), (1, 128)))
    return {"hidden": hidden, "weights": weights, "pattern": pattern, "row_of_slot": row_of_slot, "cotangent": cotangent}


def source_slots(pattern, row_of_slot):
    total = row_of_slot.shape[0]
    slots = jnp.arange(total, dtype=jnp.int32)
    equal = (row_of_slot[None, None, :] == pattern[:, :, None]).astype(jnp.int32)
    return lax.optimization_barrier(jnp.sum(equal * slots[None, None, :], axis=2)).astype(jnp.int32)

def reference(hidden, weights, pattern, row_of_slot, cotangent):
    sources = source_slots(pattern, row_of_slot)
    all_rows = hidden.shape[0]
    groups = all_rows // TOK
    blocks = hidden.reshape(all_rows, NB, BS)
    grads = jnp.transpose(cotangent.reshape(all_rows, NB, BS), (1, 0, 2))
    scale = 1.0 / jnp.sqrt(jnp.float32(TOKENS))

    def per_slot(carry, inputs):
        weight_blocks, source_row, grad_block = inputs
        taken = blocks[:, source_row, :]
        flat_taken = taken.reshape(all_rows, K * BS).astype(jnp.float32)
        flat_weights = weight_blocks.reshape(K * BS, 2 * BS).astype(jnp.float32)
        both = jnp.dot(flat_taken, flat_weights)
        gate = both[:, :BS]
        upper = both[:, BS:]
        sigma = jax.nn.sigmoid(gate)
        result = (gate * sigma * upper).astype(jnp.bfloat16)
        gradf = grad_block.astype(jnp.float32)
        dgate = gradf * upper * sigma * (1.0 + gate * (1.0 - sigma))
        dup = gradf * gate * sigma
        dboth = jnp.concatenate([dgate, dup], axis=1).astype(jnp.bfloat16)
        dboth_f = dboth.astype(jnp.float32)
        partial_value = jnp.einsum('to,kbo->tkb', dboth_f, weight_blocks.astype(jnp.float32)).astype(jnp.bfloat16)
        carry = carry.at[:, source_row, :].add(partial_value.astype(jnp.float32))
        terms = jnp.einsum('gtc,gto->gco', flat_taken.reshape(groups, TOK, K * BS), dboth_f.reshape(groups, TOK, 2 * BS))
        terms = terms.astype(jnp.bfloat16).astype(jnp.float32)
        wgrad = (lax.optimization_barrier(jnp.sum(terms, axis=0)) * scale).astype(jnp.bfloat16).reshape(K, BS, 2 * BS)
        return (carry, (result, wgrad))
    start = jnp.zeros((all_rows, NB, BS), jnp.float32)
    carry, (results, wgrads) = lax.scan(per_slot, start, (weights, sources, grads))
    output = jnp.transpose(results, (1, 0, 2)).reshape(all_rows, NB * BS)
    input_grad = carry.reshape(all_rows, NB * BS).astype(jnp.bfloat16)
    return (output, input_grad, wgrads)
```

```python
import math

import jax
import jax.numpy as jnp
from jax import lax
from jax.experimental import pallas as pl
from jax.experimental.pallas import tpu as pltpu
from jax.sharding import PartitionSpec as P

BF = jnp.bfloat16
F32 = jnp.float32
SIDE = 8


def device_at(y, z, core):
    return (y * SIDE + z) * 2 + core


GROUPS_NEAR = [[device_at(y, z, 0) for y in range(SIDE)] for z in range(SIDE)] + [
    [device_at(y, z, 1) for z in range(SIDE)] for y in range(SIDE)
]
GROUPS_FAR = [[device_at(y, z, 0) for z in range(SIDE)] for y in range(SIDE)] + [
    [device_at(y, z, 1) for y in range(SIDE)] for z in range(SIDE)
]
SWAP = [(i, i ^ 1) for i in range(2 * SIDE * SIDE)]


def swap_cores(value):
    return lax.ppermute(value, "blk", SWAP)


def exchange(value, groups):
    return lax.all_to_all(value, "blk", 0, 0, axis_index_groups=groups, tiled=True)


def block_kernel(idx, gathered, weights, turned, grads, out, kept, dense):
    row = pl.program_id(0)
    blocks = weights.shape[1] // 128
    flat = blocks * 128

    @pl.when(row == 0)
    def _():
        dense[...] = jnp.zeros_like(dense)

    for k in range(blocks):
        kept[0, :, k * 128 : (k + 1) * 128] = gathered[idx[row * blocks + k]]
    both = jnp.dot(kept[0, :, :flat], weights[0], preferred_element_type=F32)
    gate = both[:, :128]
    upper = both[:, 128:]
    sigma = jax.nn.sigmoid(gate)
    out[0] = (gate * sigma * upper).astype(BF)
    gradf = grads[0].astype(F32)
    dgate = gradf * upper * sigma * (1.0 + gate * (1.0 - sigma))
    dup = gradf * gate * sigma
    dboth = jnp.concatenate([dgate, dup], axis=1).astype(BF)
    kept[0, :, flat:] = dboth
    partial = jnp.dot(dboth, turned[0], preferred_element_type=F32).astype(BF)
    for k in range(blocks):
        at = idx[row * blocks + k]
        total = dense[at].astype(F32) + partial[:, k * 128 : (k + 1) * 128].astype(F32)
        dense[at] = total.astype(BF)


def run_blocks(idx, gathered, weights, turned, grads):
    rows, flat = weights.shape[:2]
    tokens = grads.shape[1]
    return pl.pallas_call(
        block_kernel,
        grid_spec=pltpu.PrefetchScalarGridSpec(
            num_scalar_prefetch=1,
            grid=(rows,),
            in_specs=[
                pl.BlockSpec(gathered.shape, lambda r, i: (0, 0, 0)),
                pl.BlockSpec((1, flat, 256), lambda r, i: (r, 0, 0)),
                pl.BlockSpec((1, 256, flat), lambda r, i: (r, 0, 0)),
                pl.BlockSpec((1, tokens, 128), lambda r, i: (r, 0, 0)),
            ],
            out_specs=[
                pl.BlockSpec((1, tokens, 128), lambda r, i: (r, 0, 0)),
                pl.BlockSpec((1, tokens, flat + 256), lambda r, i: (r, 0, 0)),
                pl.BlockSpec(gathered.shape, lambda r, i: (0, 0, 0)),
            ],
        ),
        out_shape=[
            jax.ShapeDtypeStruct((rows, tokens, 128), BF),
            jax.ShapeDtypeStruct((rows, tokens, flat + 256), BF),
            jax.ShapeDtypeStruct(gathered.shape, BF),
        ],
        compiler_params=pltpu.CompilerParams(
            dimension_semantics=("arbitrary",), vmem_limit_bytes=44 * 1024 * 1024
        ),
        cost_estimate=pl.CostEstimate(
            flops=4 * rows * tokens * flat * 256,
            bytes_accessed=4 * rows * flat * 256 + 4 * gathered.size,
            transcendentals=rows * tokens * 128,
        ),
    )(idx, gathered, weights, turned, grads)


def local(hidden, weights, pattern, row_of_slot, cotangent):
    tokens = hidden.shape[0]
    half = tokens // 2
    owned, per_row, width = weights.shape[:3]
    flat = per_row * width
    me = lax.axis_index("blk")
    core = me % 2
    other = me + 1 - 2 * core
    first = core == 0

    def of_core(value, which):
        return lax.dynamic_slice_in_dim(value, which * half, half, 0)

    def split(value):
        return jnp.transpose(value.reshape(half, owned, width), (1, 0, 2))

    with jax.named_scope("swap_tokens"):
        sent = jnp.stack([of_core(hidden, 1 - core), of_core(cotangent, 1 - core)])
        came = swap_cores(sent)
        mine, theirs = split(of_core(hidden, core)), split(came[0])
        chip_blocks = jnp.where(
            first, jnp.concatenate([mine, theirs]), jnp.concatenate([theirs, mine])
        )
        grads = jnp.concatenate([split(of_core(cotangent, core)), split(came[1])])
    with jax.named_scope("gather_near"):
        near = exchange(
            jnp.broadcast_to(chip_blocks[None], (SIDE,) + chip_blocks.shape), GROUPS_NEAR
        )
    with jax.named_scope("gather_far"):
        gathered = lax.all_gather(near, "blk", axis_index_groups=GROUPS_FAR, tiled=True)
        gathered = gathered.reshape(SIDE * SIDE * 2 * owned, half, width)
    with jax.named_scope("swap_weights"):
        partner = swap_cores(weights)
        all_weights = jnp.concatenate([weights, partner]).reshape(2 * owned, flat, 2 * width)
        turned = jnp.transpose(all_weights, (0, 2, 1))
    with jax.named_scope("sources"):
        wanted = jnp.concatenate(
            [
                lax.dynamic_slice_in_dim(pattern, me * owned, owned, 0),
                lax.dynamic_slice_in_dim(pattern, other * owned, owned, 0),
            ]
        )
        slots = jnp.arange(row_of_slot.shape[0], dtype=jnp.int32)
        equal = row_of_slot[None, None, :] == wanted[:, :, None]
        source = jnp.sum(jnp.where(equal, slots[None, None, :], 0), axis=2)
        chip, inside = source // (2 * owned), source % (2 * owned)
        chip_y, chip_z = chip // SIDE, chip % SIDE
        place = jnp.where(first, chip_z * SIDE + chip_y, chip_y * SIDE + chip_z)
        idx = (place * (2 * owned) + inside).reshape(-1)

    with jax.named_scope("blocks"):
        result, kept, dense = run_blocks(idx, gathered, all_weights, turned, grads)

    def rejoin(keep, came):
        low = jnp.where(first, keep, came)
        high = jnp.where(first, came, keep)
        whole = jnp.stack([low, high])
        return jnp.transpose(whole, (0, 2, 1, 3)).reshape(tokens, owned * width)

    with jax.named_scope("weight_terms"):
        came = swap_cores(kept[owned:])
        both_halves = jnp.stack([kept[:owned], came])
        terms = jnp.einsum(
            "hjtb,hjto->jbo",
            both_halves[..., :flat],
            both_halves[..., flat:],
            preferred_element_type=F32,
        ).astype(BF)
        summed = lax.psum_scatter(
            terms.reshape(owned, per_row, width, 2 * width), "dp", scatter_dimension=2, tiled=True
        )
        scale = 1.0 / math.sqrt(tokens * lax.axis_size("dp"))
        weight_grad = (summed.astype(F32) * scale).astype(BF)

    with jax.named_scope("reduce_far"):
        pieces = exchange(dense.reshape(SIDE, SIDE * 2 * owned * half, width), GROUPS_FAR)
        column = jnp.sum(pieces.astype(F32), axis=0).astype(BF)
    with jax.named_scope("reduce_near"):
        pieces = exchange(column.reshape(SIDE, 2 * owned * half, width), GROUPS_NEAR)
        total = jnp.sum(pieces.astype(F32), axis=0).astype(BF)
        total = total.reshape(2, owned, half, width)
    with jax.named_scope("swap_back"):
        keep = jnp.where(first, total[0], total[1])
        came = swap_cores(jnp.where(first, total[1], total[0]))
        input_grad = rejoin(keep, came)
        output = rejoin(result[:owned], swap_cores(result[owned:]))
    return (output, input_grad, weight_grad)


def solution(mesh):
    placed = (P("dp", "blk"), P("blk", None, None, None), P(), P(), P("dp", "blk"))
    return jax.shard_map(
        local,
        mesh=mesh,
        in_specs=placed,
        out_specs=(P("dp", "blk"), P("dp", "blk"), P("blk", None, "dp", None)),
        check_vma=False,
    )
```

```python
import math

import jax
import jax.numpy as jnp
from jax import lax
from jax.experimental import pallas as pl
from jax.experimental.pallas import tpu as pltpu
from jax.sharding import PartitionSpec as P

BF = jnp.bfloat16
F32 = jnp.float32
SIDE = 8
DEVICES = 2 * SIDE * SIDE
BOTH = ("blk", "dp")


def device_at(y, z, core):
    return (y % SIDE * SIDE + z % SIDE) * 2 + core


GROUPS_NEAR = [[device_at(y, z, 0) for y in range(SIDE)] for z in range(SIDE)] + [
    [device_at(y, z, 1) for z in range(SIDE)] for y in range(SIDE)
]
SWAP = [(i, i ^ 1) for i in range(DEVICES)]


def far_shift(value, by):
    pairs = []
    for y in range(SIDE):
        for z in range(SIDE):
            pairs.append((device_at(y, z, 0), device_at(y, z + by, 0)))
            pairs.append((device_at(y, z, 1), device_at(y + by, z, 1)))
    return lax.ppermute(value, "blk", pairs)


def swap_cores(value):
    return lax.ppermute(value, "blk", SWAP)


def near_exchange(value):
    return lax.all_to_all(value, "blk", 0, 0, axis_index_groups=GROUPS_NEAR, tiled=True)


def far_gather(own):
    middle = own.shape[0] // 2
    back2 = far_shift(own, 2)
    ahead2 = far_shift(own, -2)
    back1 = far_shift(own, 1)
    ahead1 = far_shift(own, -1)
    back3 = far_shift(back2, 1)
    ahead3 = far_shift(ahead2, -1)
    low = far_shift(back2[:middle], 2)
    high = far_shift(ahead2[middle:], -2)
    return own, ahead1, ahead2, ahead3, low, high, back3, back2, back1


def far_reduce(own, to31, to2, to4_low, to4_high, to57, to6):
    got31 = far_shift(to31, 1)
    got57 = far_shift(to57, -1)
    got4_low = far_shift(to4_low, 2)
    got4_high = far_shift(to4_high, -2)
    size = own.shape[0]
    middle = size // 2

    def add(*values):
        return sum(value.astype(F32) for value in values).astype(BF)

    sum2 = jnp.concatenate(
        [
            add(to2[:middle], got31[:middle], got4_low),
            add(to2[middle:], got31[middle:size]),
        ]
    )
    sum6 = jnp.concatenate(
        [
            add(to6[:middle], got57[:middle]),
            add(to6[middle:], got57[middle:size], got4_high),
        ]
    )
    got2 = far_shift(sum2, 2)
    got6 = far_shift(sum6, -2)
    return add(own, got31[size:], got57[size:], got2, got6)


def block_kernel(core, idx, *refs):
    chunks = refs[:9]
    weight_refs = refs[9:11]
    grads, out = refs[11:13]
    terms = refs[13:20]
    packed_out = refs[20]
    gathered, dense, kept, packed, in_sems, out_sems, pack_sems = refs[21:]
    rows, tokens, wide = kept.shape
    flat = wide - 256
    blocks = flat // 128
    side = chunks[0].shape[0]
    half = side // 2
    places = [(d * side, side) for d in range(4)]
    places += [(4 * side, half), (4 * side + half, half)]
    places += [(d * side, side) for d in range(5, 8)]

    loads = [
        pltpu.make_async_copy(ref, gathered.at[pl.ds(at, size)], in_sems.at[i])
        for i, (ref, (at, size)) in enumerate(zip(chunks, places))
    ]
    for copy in loads:
        copy.start()
    dense[...] = jnp.zeros_like(dense)
    for copy in loads:
        copy.wait()
    for row in range(rows):
        for k in range(blocks):
            kept[row, :, k * 128 : (k + 1) * 128] = gathered[idx[row * blocks + k]]
    for row in range(rows):
        weights = weight_refs[row // 2].at[row % 2]
        both = jnp.dot(kept[row, :, :flat], weights[...], preferred_element_type=F32)
        gate = both[:, :128]
        upper = both[:, 128:]
        sigma = jax.nn.sigmoid(gate)
        out[row] = (gate * sigma * upper).astype(BF)
        gradf = grads[row].astype(F32)
        dgate = gradf * upper * sigma * (1.0 + gate * (1.0 - sigma))
        dup = gradf * gate * sigma
        kept[row, :, flat:] = jnp.concatenate([dgate, dup], axis=1).astype(BF)
    for row in range(rows):
        weights = weight_refs[row // 2].at[row % 2]
        partial = lax.dot_general(
            kept[row, :, flat:],
            weights[...],
            (((1,), (1,)), ((), ())),
            preferred_element_type=F32,
        ).astype(BF)
        for start in range(0, blocks, 6):
            span = range(start, min(start + 6, blocks))
            values = [partial[:, k * 128 : (k + 1) * 128] for k in span]
            places_of = [idx[row * blocks + k] for k in span]
            if row >= rows // 2:
                values = [
                    (dense[at].astype(F32) + value.astype(F32)).astype(BF)
                    for at, value in zip(places_of, values)
                ]
            for at, value in zip(places_of, values):
                dense[at] = value
    own, to31, to2, to4_low, to4_high, to57, to6 = terms
    pieces = [
        (to31.at[pl.ds(0, side)], 3),
        (to57.at[pl.ds(0, side)], 6),
        (to4_low, 4),
        (to4_high, 5),
        (to31.at[pl.ds(side, side)], 1),
        (to57.at[pl.ds(side, side)], 8),
        (to2, 2),
        (to6, 7),
        (own, 0),
    ]
    stores = [
        pltpu.make_async_copy(
            dense.at[pl.ds(places[at][0], places[at][1])], ref, out_sems.at[i]
        )
        for i, (ref, at) in enumerate(pieces)
    ]
    for copy in stores:
        copy.start()
    shards = packed.shape[0] // 2
    part = 128 // shards
    for pair in range(2):
        base = lax.rem(core[0] + pair, 2) * shards
        for k in range(blocks):
            cut = slice(k * 128, (k + 1) * 128)
            turned = jnp.concatenate(
                [kept[2 * pair, :, cut], kept[2 * pair + 1, :, cut]], axis=0
            ).T
            for x in range(shards):
                packed[pair * shards + x, k * part : (k + 1) * part, :] = turned[
                    x * part : (x + 1) * part
                ]
        for row in range(2):
            for side in range(2):
                value = kept[2 * pair + row, :, flat + side * 128 : flat + (side + 1) * 128]
                at = blocks * part + (2 * row + side) * tokens
                for x in range(shards):
                    packed[pair * shards + x, at : at + tokens, :] = value
        copy = pltpu.make_async_copy(
            packed.at[pl.ds(pair * shards, shards)],
            packed_out.at[pl.ds(base, shards)],
            pack_sems.at[pair],
        )
        copy.start()
        stores.append(copy)
    for copy in stores:
        copy.wait()


def run_blocks(core, idx, chunks, weights, other_weights, grads, shards):
    rows, tokens = grads.shape[:2]
    flat = weights.shape[1]
    outside = pl.BlockSpec(memory_space=pl.ANY)
    whole = pl.BlockSpec(memory_space=pltpu.VMEM)
    scalars = pl.BlockSpec(memory_space=pltpu.SMEM)
    side = chunks[0].shape[0]
    total = SIDE * side
    lengths = (side, 2 * side, side, side // 2, side // 2, 2 * side, side)
    packed = (2 * shards, flat // shards + 4 * tokens, 128)
    return pl.pallas_call(
        block_kernel,
        in_specs=[scalars] * 2 + [outside] * 9 + [whole] * 3,
        out_specs=[whole] + [outside] * 8,
        out_shape=[jax.ShapeDtypeStruct((rows, tokens, 128), BF)]
        + [jax.ShapeDtypeStruct((n,) + chunks[0].shape[1:], BF) for n in lengths]
        + [jax.ShapeDtypeStruct(packed, BF)],
        scratch_shapes=[
            pltpu.VMEM((total, tokens, 128), BF),
            pltpu.VMEM((total, tokens, 128), BF),
            pltpu.VMEM((rows, tokens, flat + 256), BF),
            pltpu.VMEM(packed, BF),
            pltpu.SemaphoreType.DMA((9,)),
            pltpu.SemaphoreType.DMA((9,)),
            pltpu.SemaphoreType.DMA((2,)),
        ],
        compiler_params=pltpu.CompilerParams(vmem_limit_bytes=56 * 1024 * 1024),
        cost_estimate=pl.CostEstimate(
            flops=4 * rows * tokens * flat * 256,
            bytes_accessed=2 * rows * flat * 256 + 4 * total * tokens * 128,
            transcendentals=rows * tokens * 128,
        ),
    )(core, idx, *chunks, weights, other_weights, grads)


def weight_kernel(scale, packed, out, total, right):
    sources, height = packed.shape[:2]
    blocks, part = out.shape[1:3]
    flat = blocks * part
    tokens = (height - flat) // 4
    right[...] = jnp.zeros_like(right)
    for step in range(sources // 2):
        for i in range(2):
            for row in range(2):
                for side in range(2):
                    at = flat + (2 * row + side) * tokens
                    right[
                        (2 * i + row) * tokens : (2 * i + row + 1) * tokens,
                        row * 256 + side * 128 : row * 256 + (side + 1) * 128,
                    ] = packed[2 * step + i, at : at + tokens, :]
        left = jnp.concatenate([packed[2 * step, :flat, :], packed[2 * step + 1, :flat, :]], axis=1)
        product = jnp.dot(left, right[...], preferred_element_type=F32)
        if step == 0:
            total[...] = product
        else:
            total[...] += product
    for row in range(2):
        for k in range(blocks):
            value = total[k * part : (k + 1) * part, row * 256 : (row + 1) * 256]
            out[row, k] = (value * scale).astype(BF)


def run_weights(packed, blocks, part, scale):
    sources, height = packed.shape[:2]
    return pl.pallas_call(
        lambda *refs: weight_kernel(scale, *refs),
        in_specs=[pl.BlockSpec(memory_space=pltpu.VMEM)],
        out_specs=pl.BlockSpec(memory_space=pltpu.VMEM),
        out_shape=jax.ShapeDtypeStruct((2, blocks, part, 256), BF),
        scratch_shapes=[
            pltpu.VMEM((blocks * part, 512), F32),
            pltpu.VMEM((256, 512), BF),
        ],
        compiler_params=pltpu.CompilerParams(vmem_limit_bytes=16 * 1024 * 1024),
        cost_estimate=pl.CostEstimate(
            flops=2 * blocks * part * 512 * sources * 128,
            bytes_accessed=2 * sources * height * 128 + 4 * blocks * part * 256,
            transcendentals=0,
        ),
    )(packed)


def local(hidden, weights, pattern, row_of_slot, cotangent):
    tokens = hidden.shape[0]
    half = tokens // 2
    owned, per_row, width = weights.shape[:3]
    flat = per_row * width
    shards = lax.axis_size("dp")
    me = lax.axis_index("blk")
    core = me % 2
    other = me + 1 - 2 * core
    first = core == 0

    def choose(value, mine):
        low, high = value[:half], value[half:]
        return jnp.where(first == mine, low, high)

    def split(value):
        return jnp.transpose(value.reshape(half, owned, width), (1, 0, 2))

    with jax.named_scope("swap_tokens"):
        came = swap_cores(jnp.stack([choose(hidden, False), choose(cotangent, False)]))
        mine, theirs = split(choose(hidden, True)), split(came[0])
        chip_blocks = jnp.where(
            first, jnp.concatenate([mine, theirs]), jnp.concatenate([theirs, mine])
        )
        grads = jnp.concatenate([split(choose(cotangent, True)), split(came[1])])
    with jax.named_scope("gather_near"):
        near = near_exchange(jnp.broadcast_to(chip_blocks[None], (SIDE,) + chip_blocks.shape))
        near = near.reshape(SIDE * 2 * owned, half, width)
    with jax.named_scope("gather_far"):
        chunks = far_gather(near)
    with jax.named_scope("swap_weights"):
        ready, _ = lax.optimization_barrier((weights, near))
        other_weights = swap_cores(ready)
    with jax.named_scope("sources"):
        wanted = jnp.concatenate(
            [
                lax.dynamic_slice_in_dim(pattern, me * owned, owned, 0),
                lax.dynamic_slice_in_dim(pattern, other * owned, owned, 0),
            ]
        )
        slots = jnp.arange(row_of_slot.shape[0], dtype=jnp.int32)
        equal = row_of_slot[None, None, :] == wanted[:, :, None]
        source = jnp.sum(jnp.where(equal, slots[None, None, :], 0), axis=2)
        chip, inside = source // (2 * owned), source % (2 * owned)
        chip_y, chip_z = chip // SIDE, chip % SIDE
        my_y, my_z = me // (2 * SIDE), me // 2 % SIDE
        distance = jnp.where(first, chip_z - my_z, chip_y - my_y) % SIDE
        place = distance * SIDE + jnp.where(first, chip_y, chip_z)
        idx = (place * (2 * owned) + inside).reshape(-1)

    with jax.named_scope("blocks"):
        result, *terms, packed = run_blocks(
            core.reshape(1),
            idx,
            chunks,
            weights.reshape(owned, flat, 2 * width),
            other_weights.reshape(owned, flat, 2 * width),
            grads,
            shards,
        )

    def rejoin(keep, came):
        low = jnp.where(first, keep, came)
        high = jnp.where(first, came, keep)
        whole = jnp.stack([low, high])
        return jnp.transpose(whole, (0, 2, 1, 3)).reshape(tokens, owned * width)

    with jax.named_scope("reduce_far"):
        column = far_reduce(*terms)
    with jax.named_scope("weight_grad"):
        size = 2 * shards
        groups = [[i * size + j for j in range(size)] for i in range(DEVICES // 2)]
        packed = lax.all_to_all(packed, BOTH, 0, 0, axis_index_groups=groups, tiled=True)
        scale = 1.0 / math.sqrt(tokens * shards)
    with jax.named_scope("reduce_near"):
        column, packed = lax.optimization_barrier((column, packed))
        weight_grad = run_weights(packed, per_row, width // shards, scale)
        pieces = near_exchange(column.reshape(SIDE, 2 * owned * half, width))
        total = jnp.sum(pieces.astype(F32), axis=0).astype(BF)
        total = total.reshape(2, owned, half, width)
    with jax.named_scope("swap_back"):
        keep = jnp.where(first, total[0], total[1])
        came = swap_cores(jnp.where(first, total[1], total[0]))
        input_grad = rejoin(keep, came)
        output = rejoin(result[:owned], swap_cores(result[owned:]))
    return (output, input_grad, weight_grad)


def solution(mesh):
    placed = (P("dp", "blk"), P("blk", None, None, None), P(), P(), P("dp", "blk"))
    return jax.shard_map(
        local,
        mesh=mesh,
        in_specs=placed,
        out_specs=(P("dp", "blk"), P("dp", "blk"), P("blk", None, "dp", None)),
        check_vma=False,
    )
```

```python
import math

import jax
import jax.numpy as jnp
from jax import lax
from jax.experimental import pallas as pl
from jax.experimental.pallas import tpu as pltpu
from jax.sharding import PartitionSpec as P

BF = jnp.bfloat16
F32 = jnp.float32
SIDE = 8
DEVICES = 2 * SIDE * SIDE
BOTH = ("blk", "dp")


def device_at(y, z, core):
    return (y % SIDE * SIDE + z % SIDE) * 2 + core


GROUPS_NEAR = [[device_at(y, z, 0) for y in range(SIDE)] for z in range(SIDE)] + [
    [device_at(y, z, 1) for z in range(SIDE)] for y in range(SIDE)
]
SWAP = [(i, i ^ 1) for i in range(DEVICES)]


def far_shift(value, by):
    pairs = []
    for y in range(SIDE):
        for z in range(SIDE):
            here = z + by * (1 - 2 * (z % 2))
            pairs.append((device_at(y, z, 0), device_at(y, here, 0)))
            here = y + by * (1 - 2 * (y % 2))
            pairs.append((device_at(y, z, 1), device_at(here, z, 1)))
    return lax.ppermute(value, "blk", pairs)


def swap_cores(value):
    return lax.ppermute(value, "blk", SWAP)


def near_exchange(value):
    return lax.all_to_all(value, "blk", 0, 0, axis_index_groups=GROUPS_NEAR, tiled=True)


def far_gather(own):
    at6 = far_shift(own, 2)
    at2 = far_shift(own, -2)
    at1 = far_shift(own, 1)
    at7 = far_shift(own, -1)
    at4 = far_shift(at6, 2)
    at3 = far_shift(at6, 1)
    at5 = far_shift(at2, -1)
    return own, at1, at2, at3, at4, at5, at6, at7


def far_reduce(own, to31, to57, to4, to2, to6):
    size = own.shape[0]
    got31 = far_shift(to31, 1)
    got57 = far_shift(to57, -1)
    got4 = far_shift(to4, 2)

    def add(*values):
        return sum(value.astype(F32) for value in values).astype(BF)

    got6 = far_shift(add(to6, got31[:size]), -2)
    got2 = far_shift(add(to2, got57[:size], got4), 2)
    early = lax.optimization_barrier(
        own.astype(F32) + got31[size:].astype(F32) + got57[size:].astype(F32)
    )
    return add(early, got2, got6)


def block_kernel(core, idx, *refs):
    chunks = refs[:8]
    weights_here, weights_there, grads, out = refs[8:12]
    terms = refs[12:18]
    packed_out = refs[18]
    gathered, dense, kept, packed, weights, in_sems, out_sems, pack_sems, weight_sems = refs[19:]
    rows, tokens, wide = kept.shape
    flat = wide - 256
    blocks = flat // 128
    side = chunks[0].shape[0]

    def place(distance):
        return pl.ds(distance * side, side)

    loads = [
        pltpu.make_async_copy(ref, gathered.at[place(i)], in_sems.at[i])
        for i, ref in enumerate(chunks)
    ]
    weight_loads = [
        pltpu.make_async_copy(weights_here.at[i], weights.at[i], weight_sems.at[i])
        for i in range(rows // 2)
    ]
    for copy in loads + weight_loads:
        copy.start()
    dense[...] = jnp.zeros_like(dense)
    for copy in loads:
        copy.wait()
    for row in range(rows):
        for k in range(blocks):
            kept[row, :, k * 128 : (k + 1) * 128] = gathered[idx[row * blocks + k]]
    order = [2, 3, 0, 1]
    for row in order:
        if row < 2:
            weight_loads[row].wait()
        matrix = weights[row] if row < 2 else weights_there[row - 2]
        both = jnp.dot(kept[row, :, :flat], matrix, preferred_element_type=F32)
        gate = both[:, :128]
        upper = both[:, 128:]
        sigma = jax.nn.sigmoid(gate)
        out[row] = (gate * sigma * upper).astype(BF)
        gradf = grads[row].astype(F32)
        dgate = gradf * upper * sigma * (1.0 + gate * (1.0 - sigma))
        dup = gradf * gate * sigma
        kept[row, :, flat:] = jnp.concatenate([dgate, dup], axis=1).astype(BF)
    for row in order:
        matrix = weights[row] if row < 2 else weights_there[row - 2]
        partial = lax.dot_general(
            kept[row, :, flat:],
            matrix,
            (((1,), (1,)), ((), ())),
            preferred_element_type=F32,
        ).astype(BF)
        for start in range(0, blocks, 6):
            span = range(start, min(start + 6, blocks))
            values = [partial[:, k * 128 : (k + 1) * 128] for k in span]
            places_of = [idx[row * blocks + k] for k in span]
            if row < 2:
                values = [
                    (dense[at].astype(F32) + value.astype(F32)).astype(BF)
                    for at, value in zip(places_of, values)
                ]
            for at, value in zip(places_of, values):
                dense[at] = value
    own, to31, to57, to4, to2, to6 = terms
    pieces = [
        (to31.at[place(0)], place(3)),
        (to57.at[place(0)], place(5)),
        (to4, place(4)),
        (to31.at[place(1)], place(1)),
        (to57.at[place(1)], place(7)),
        (to2, place(2)),
        (to6, place(6)),
        (own, place(0)),
    ]
    stores = [
        pltpu.make_async_copy(dense.at[at], ref, out_sems.at[i])
        for i, (ref, at) in enumerate(pieces)
    ]
    for copy in stores:
        copy.start()
    shards = packed.shape[0] // 2
    part = 128 // shards
    for pair in range(2):
        base = lax.rem(core[0] + pair, 2) * shards
        for k in range(blocks):
            cut = slice(k * 128, (k + 1) * 128)
            turned = jnp.concatenate(
                [kept[2 * pair, :, cut], kept[2 * pair + 1, :, cut]], axis=0
            ).T
            for x in range(shards):
                packed[pair * shards + x, k * part : (k + 1) * part, :] = turned[
                    x * part : (x + 1) * part
                ]
        for row in range(2):
            for wing in range(2):
                value = kept[2 * pair + row, :, flat + wing * 128 : flat + (wing + 1) * 128]
                at = blocks * part + (2 * row + wing) * tokens
                for x in range(shards):
                    packed[pair * shards + x, at : at + tokens, :] = value
        copy = pltpu.make_async_copy(
            packed.at[pl.ds(pair * shards, shards)],
            packed_out.at[pl.ds(base, shards)],
            pack_sems.at[pair],
        )
        copy.start()
        stores.append(copy)
    for copy in stores:
        copy.wait()


def run_blocks(core, idx, chunks, weights, other_weights, grads, shards):
    rows, tokens = grads.shape[:2]
    flat = weights.shape[1]
    outside = pl.BlockSpec(memory_space=pl.ANY)
    whole = pl.BlockSpec(memory_space=pltpu.VMEM)
    scalars = pl.BlockSpec(memory_space=pltpu.SMEM)
    side = chunks[0].shape[0]
    total = SIDE * side
    lengths = (side, 2 * side, 2 * side, side, side, side)
    packed = (2 * shards, flat // shards + 4 * tokens, 128)
    return pl.pallas_call(
        block_kernel,
        in_specs=[scalars] * 2 + [outside] * 9 + [whole] * 2,
        out_specs=[whole] + [outside] * 7,
        out_shape=[jax.ShapeDtypeStruct((rows, tokens, 128), BF)]
        + [pltpu.HBM((n,) + chunks[0].shape[1:], BF) for n in lengths]
        + [pltpu.HBM(packed, BF)],
        scratch_shapes=[
            pltpu.VMEM((total, tokens, 128), BF),
            pltpu.VMEM((total, tokens, 128), BF),
            pltpu.VMEM((rows, tokens, flat + 256), BF),
            pltpu.VMEM(packed, BF),
            pltpu.VMEM(weights.shape, BF),
            pltpu.SemaphoreType.DMA((8,)),
            pltpu.SemaphoreType.DMA((8,)),
            pltpu.SemaphoreType.DMA((2,)),
            pltpu.SemaphoreType.DMA((2,)),
        ],
        compiler_params=pltpu.CompilerParams(vmem_limit_bytes=40 * 1024 * 1024),
        cost_estimate=pl.CostEstimate(
            flops=4 * rows * tokens * flat * 256,
            bytes_accessed=2 * rows * flat * 256 + 4 * total * tokens * 128,
            transcendentals=rows * tokens * 128,
        ),
    )(
        core,
        idx,
        *chunks,
        pltpu.with_memory_space_constraint(weights, pltpu.HBM),
        other_weights,
        grads,
    )


def weight_kernel(scale, packed, out, total, right):
    sources, height = packed.shape[:2]
    blocks, part = out.shape[1:3]
    flat = blocks * part
    tokens = (height - flat) // 4
    right[...] = jnp.zeros_like(right)
    for step in range(sources // 2):
        for i in range(2):
            for row in range(2):
                for side in range(2):
                    at = flat + (2 * row + side) * tokens
                    right[
                        (2 * i + row) * tokens : (2 * i + row + 1) * tokens,
                        row * 256 + side * 128 : row * 256 + (side + 1) * 128,
                    ] = packed[2 * step + i, at : at + tokens, :]
        left = jnp.concatenate([packed[2 * step, :flat, :], packed[2 * step + 1, :flat, :]], axis=1)
        product = jnp.dot(left, right[...], preferred_element_type=F32)
        if step == 0:
            total[...] = product
        else:
            total[...] += product
    for row in range(2):
        for k in range(blocks):
            value = total[k * part : (k + 1) * part, row * 256 : (row + 1) * 256]
            out[row, k] = (value * scale).astype(BF)


def run_weights(packed, blocks, part, scale):
    sources, height = packed.shape[:2]
    return pl.pallas_call(
        lambda *refs: weight_kernel(scale, *refs),
        in_specs=[pl.BlockSpec(memory_space=pltpu.VMEM)],
        out_specs=pl.BlockSpec(memory_space=pltpu.VMEM),
        out_shape=jax.ShapeDtypeStruct((2, blocks, part, 256), BF),
        scratch_shapes=[
            pltpu.VMEM((blocks * part, 512), F32),
            pltpu.VMEM((256, 512), BF),
        ],
        compiler_params=pltpu.CompilerParams(vmem_limit_bytes=16 * 1024 * 1024),
        cost_estimate=pl.CostEstimate(
            flops=2 * blocks * part * 512 * sources * 128,
            bytes_accessed=2 * sources * height * 128 + 4 * blocks * part * 256,
            transcendentals=0,
        ),
    )(packed)


def local(hidden, weights, pattern, row_of_slot, cotangent):
    tokens = hidden.shape[0]
    half = tokens // 2
    owned, per_row, width = weights.shape[:3]
    flat = per_row * width
    shards = lax.axis_size("dp")
    me = lax.axis_index("blk")
    core = me % 2
    other = me + 1 - 2 * core
    first = core == 0

    def split(value):
        return jnp.transpose(value.reshape(half, owned, width), (1, 0, 2))

    with jax.named_scope("swap_tokens"):
        both = jnp.stack([hidden, cotangent])
        low, high = both[:, :half], both[:, half:]
        came = swap_cores(jnp.where(first, high, low))
        stays = jnp.where(first, low, high)
        mine, theirs = split(stays[0]), split(came[0])
        chip_blocks = jnp.where(
            first, jnp.concatenate([mine, theirs]), jnp.concatenate([theirs, mine])
        )
        grads = jnp.concatenate([split(stays[1]), split(came[1])])
    with jax.named_scope("gather_near"):
        near = near_exchange(jnp.broadcast_to(chip_blocks[None], (SIDE,) + chip_blocks.shape))
        near = near.reshape(SIDE * 2 * owned, half, width)
    with jax.named_scope("gather_far"):
        chunks = far_gather(near)
    with jax.named_scope("swap_weights"):
        ready, _ = lax.optimization_barrier((weights, near))
        other_weights = swap_cores(ready)
    with jax.named_scope("sources"):
        wanted = jnp.concatenate(
            [
                lax.dynamic_slice_in_dim(pattern, me * owned, owned, 0),
                lax.dynamic_slice_in_dim(pattern, other * owned, owned, 0),
            ]
        )
        slots = jnp.arange(row_of_slot.shape[0], dtype=jnp.int32)
        equal = row_of_slot[None, None, :] == wanted[:, :, None]
        source = jnp.sum(jnp.where(equal, slots[None, None, :], 0), axis=2)
        chip, inside = source // (2 * owned), source % (2 * owned)
        chip_y, chip_z = chip // SIDE, chip % SIDE
        my_y, my_z = me // (2 * SIDE), me // 2 % SIDE
        far = jnp.where(first, my_z, my_y)
        distance = (jnp.where(first, chip_z, chip_y) - far) * (1 - 2 * (far % 2)) % SIDE
        place = distance * SIDE + jnp.where(first, chip_y, chip_z)
        idx = (place * (2 * owned) + inside).reshape(-1)

    with jax.named_scope("blocks"):
        result, *terms, packed = run_blocks(
            core.reshape(1),
            idx,
            chunks,
            weights.reshape(owned, flat, 2 * width),
            other_weights.reshape(owned, flat, 2 * width),
            grads,
            shards,
        )

    def rejoin(keep, came):
        low = jnp.where(first, keep, came)
        high = jnp.where(first, came, keep)
        whole = jnp.stack([low, high])
        return jnp.transpose(whole, (0, 2, 1, 3)).reshape(tokens, owned * width)

    with jax.named_scope("reduce_far"):
        column = far_reduce(*terms)
    with jax.named_scope("weight_grad"):
        size = 2 * shards
        groups = [[i * size + j for j in range(size)] for i in range(DEVICES // 2)]
        packed = lax.all_to_all(packed, BOTH, 0, 0, axis_index_groups=groups, tiled=True)
        scale = 1.0 / math.sqrt(tokens * shards)
    with jax.named_scope("reduce_near"):
        column, packed = lax.optimization_barrier((column, packed))
        weight_grad = run_weights(packed, per_row, width // shards, scale)
        pieces = near_exchange(column.reshape(SIDE, 2 * owned * half, width))
        total = jnp.sum(pieces.astype(F32), axis=0).astype(BF)
        total, weight_grad = lax.optimization_barrier((total, weight_grad))
        total = total.reshape(2, owned, half, width)
    with jax.named_scope("swap_back"):
        keep = jnp.where(first, total[0], total[1])
        came = swap_cores(jnp.where(first, total[1], total[0]))
        input_grad = rejoin(keep, came)
        output = rejoin(result[:owned], swap_cores(result[owned:]))
    return (output, input_grad, weight_grad)


def solution(mesh):
    placed = (P("dp", "blk"), P("blk", None, None, None), P(), P(), P("dp", "blk"))
    return jax.shard_map(
        local,
        mesh=mesh,
        in_specs=placed,
        out_specs=(P("dp", "blk"), P("dp", "blk"), P("blk", None, "dp", None)),
        check_vma=False,
    )
```

```python
import math

import jax
import jax.numpy as jnp
from jax import lax
from jax.experimental import pallas as pl
from jax.experimental.pallas import tpu as pltpu
from jax.sharding import PartitionSpec as P

BF = jnp.bfloat16
F32 = jnp.float32
SIDE = 8
DEVICES = 2 * SIDE * SIDE
BOTH = ("blk", "dp")


def device_at(y, z, core):
    return (y % SIDE * SIDE + z % SIDE) * 2 + core


GROUPS_NEAR = [[device_at(y, z, 0) for y in range(SIDE)] for z in range(SIDE)] + [
    [device_at(y, z, 1) for z in range(SIDE)] for y in range(SIDE)
]
SWAP = [(i, i ^ 1) for i in range(DEVICES)]


def far_shift(value, by):
    pairs = []
    for y in range(SIDE):
        for z in range(SIDE):
            here = z + by * (1 - 2 * (z % 2))
            pairs.append((device_at(y, z, 0), device_at(y, here, 0)))
            here = y + by * (1 - 2 * (y % 2))
            pairs.append((device_at(y, z, 1), device_at(here, z, 1)))
    return lax.ppermute(value, "blk", pairs)


def swap_cores(value):
    return lax.ppermute(value, "blk", SWAP)


def near_exchange(value):
    return lax.all_to_all(value, "blk", 0, 0, axis_index_groups=GROUPS_NEAR, tiled=True)


def far_gather(own):
    at6 = far_shift(own, 2)
    at2 = far_shift(own, -2)
    at1 = far_shift(own, 1)
    at7 = far_shift(own, -1)
    at4 = far_shift(at6, 2)
    at3 = far_shift(at6, 1)
    at5 = far_shift(at2, -1)
    return own, at1, at2, at3, at4, at5, at6, at7


def far_reduce(own, to31, to57, to4, to2, to6):
    size = own.shape[0]
    got31 = far_shift(to31, 1)
    got57 = far_shift(to57, -1)
    got4 = far_shift(to4, 2)

    def add(*values):
        return sum(value.astype(F32) for value in values).astype(BF)

    sum6 = add(to6, got31[:size])
    to2, _ = lax.optimization_barrier((to2, sum6))
    sum2 = add(to2, got57[:size], got4)
    own, _ = lax.optimization_barrier((own, sum2))
    got6 = far_shift(sum6, -2)
    got2 = far_shift(sum2, 2)
    early = lax.optimization_barrier(
        own.astype(F32) + got31[size:].astype(F32) + got57[size:].astype(F32)
    )
    return add(early, got2, got6)


def block_kernel(core, idx, *refs):
    chunks = refs[:8]
    weights_here, weights_there, grads, out = refs[8:12]
    terms = refs[12:18]
    packed_out = refs[18]
    gathered, dense, kept, packed, weights, in_sems, out_sems, pack_sems, weight_sems = refs[19:]
    rows, tokens, wide = kept.shape
    flat = wide - 256
    blocks = flat // 128
    side = chunks[0].shape[0]

    def place(distance):
        return pl.ds(distance * side, side)

    loads = [
        pltpu.make_async_copy(ref, gathered.at[place(i)], in_sems.at[i])
        for i, ref in enumerate(chunks)
    ]
    weight_loads = [
        pltpu.make_async_copy(weights_here.at[i], weights.at[i], weight_sems.at[i])
        for i in range(rows // 2)
    ]
    for copy in loads + weight_loads:
        copy.start()
    dense[...] = jnp.zeros_like(dense)
    for copy in loads:
        copy.wait()
    for row in range(rows):
        for k in range(blocks):
            kept[row, :, k * 128 : (k + 1) * 128] = gathered[idx[row * blocks + k]]
    order = [2, 3, 0, 1]
    for row in order:
        if row < 2:
            weight_loads[row].wait()
        matrix = weights[row] if row < 2 else weights_there[row - 2]
        both = jnp.dot(kept[row, :, :flat], matrix, preferred_element_type=F32)
        gate = both[:, :128]
        upper = both[:, 128:]
        sigma = jax.nn.sigmoid(gate)
        out[row] = (gate * sigma * upper).astype(BF)
        gradf = grads[row].astype(F32)
        dgate = gradf * upper * sigma * (1.0 + gate * (1.0 - sigma))
        dup = gradf * gate * sigma
        kept[row, :, flat:] = jnp.concatenate([dgate, dup], axis=1).astype(BF)
    for row in order:
        matrix = weights[row] if row < 2 else weights_there[row - 2]
        partial = lax.dot_general(
            kept[row, :, flat:],
            matrix,
            (((1,), (1,)), ((), ())),
            preferred_element_type=F32,
        ).astype(BF)
        for start in range(0, blocks, 6):
            span = range(start, min(start + 6, blocks))
            values = [partial[:, k * 128 : (k + 1) * 128] for k in span]
            places_of = [idx[row * blocks + k] for k in span]
            if row < 2:
                values = [
                    (dense[at].astype(F32) + value.astype(F32)).astype(BF)
                    for at, value in zip(places_of, values)
                ]
            for at, value in zip(places_of, values):
                dense[at] = value
    own, to31, to57, to4, to2, to6 = terms
    pieces = [
        (to31.at[place(0)], place(3)),
        (to57.at[place(0)], place(5)),
        (to4, place(4)),
        (to31.at[place(1)], place(1)),
        (to57.at[place(1)], place(7)),
        (to2, place(2)),
        (to6, place(6)),
        (own, place(0)),
    ]
    stores = [
        pltpu.make_async_copy(dense.at[at], ref, out_sems.at[i])
        for i, (ref, at) in enumerate(pieces)
    ]
    for copy in stores:
        copy.start()
    shards = packed.shape[0] // 2
    part = 128 // shards
    for pair in range(2):
        base = lax.rem(core[0] + pair, 2) * shards
        for k in range(blocks):
            cut = slice(k * 128, (k + 1) * 128)
            turned = jnp.concatenate(
                [kept[2 * pair, :, cut], kept[2 * pair + 1, :, cut]], axis=0
            ).T
            for x in range(shards):
                packed[pair * shards + x, k * part : (k + 1) * part, :] = turned[
                    x * part : (x + 1) * part
                ]
        for row in range(2):
            for wing in range(2):
                value = kept[2 * pair + row, :, flat + wing * 128 : flat + (wing + 1) * 128]
                at = blocks * part + (2 * row + wing) * tokens
                for x in range(shards):
                    packed[pair * shards + x, at : at + tokens, :] = value
        copy = pltpu.make_async_copy(
            packed.at[pl.ds(pair * shards, shards)],
            packed_out.at[pl.ds(base, shards)],
            pack_sems.at[pair],
        )
        copy.start()
        stores.append(copy)
    for copy in stores:
        copy.wait()


def run_blocks(core, idx, chunks, weights, other_weights, grads, shards):
    rows, tokens = grads.shape[:2]
    flat = weights.shape[1]
    outside = pl.BlockSpec(memory_space=pl.ANY)
    whole = pl.BlockSpec(memory_space=pltpu.VMEM)
    scalars = pl.BlockSpec(memory_space=pltpu.SMEM)
    side = chunks[0].shape[0]
    total = SIDE * side
    lengths = (side, 2 * side, 2 * side, side, side, side)
    packed = (2 * shards, flat // shards + 4 * tokens, 128)
    return pl.pallas_call(
        block_kernel,
        in_specs=[scalars] * 2 + [outside] * 9 + [whole] * 2,
        out_specs=[whole] + [outside] * 7,
        out_shape=[jax.ShapeDtypeStruct((rows, tokens, 128), BF)]
        + [pltpu.HBM((n,) + chunks[0].shape[1:], BF) for n in lengths]
        + [pltpu.HBM(packed, BF)],
        scratch_shapes=[
            pltpu.VMEM((total, tokens, 128), BF),
            pltpu.VMEM((total, tokens, 128), BF),
            pltpu.VMEM((rows, tokens, flat + 256), BF),
            pltpu.VMEM(packed, BF),
            pltpu.VMEM(weights.shape, BF),
            pltpu.SemaphoreType.DMA((8,)),
            pltpu.SemaphoreType.DMA((8,)),
            pltpu.SemaphoreType.DMA((2,)),
            pltpu.SemaphoreType.DMA((2,)),
        ],
        compiler_params=pltpu.CompilerParams(vmem_limit_bytes=40 * 1024 * 1024),
        cost_estimate=pl.CostEstimate(
            flops=4 * rows * tokens * flat * 256,
            bytes_accessed=2 * rows * flat * 256 + 4 * total * tokens * 128,
            transcendentals=rows * tokens * 128,
        ),
    )(
        core,
        idx,
        *chunks,
        pltpu.with_memory_space_constraint(weights, pltpu.HBM),
        other_weights,
        grads,
    )


def weight_kernel(scale, packed, out, total, right):
    sources, height = packed.shape[:2]
    blocks, part = out.shape[1:3]
    flat = blocks * part
    tokens = (height - flat) // 4
    right[...] = jnp.zeros_like(right)
    for step in range(sources // 2):
        for i in range(2):
            for row in range(2):
                for side in range(2):
                    at = flat + (2 * row + side) * tokens
                    right[
                        (2 * i + row) * tokens : (2 * i + row + 1) * tokens,
                        row * 256 + side * 128 : row * 256 + (side + 1) * 128,
                    ] = packed[2 * step + i, at : at + tokens, :]
        left = jnp.concatenate([packed[2 * step, :flat, :], packed[2 * step + 1, :flat, :]], axis=1)
        product = jnp.dot(left, right[...], preferred_element_type=F32)
        if step == 0:
            total[...] = product
        else:
            total[...] += product
    for row in range(2):
        for k in range(blocks):
            value = total[k * part : (k + 1) * part, row * 256 : (row + 1) * 256]
            out[row, k] = (value * scale).astype(BF)


def run_weights(packed, blocks, part, scale):
    sources, height = packed.shape[:2]
    return pl.pallas_call(
        lambda *refs: weight_kernel(scale, *refs),
        in_specs=[pl.BlockSpec(memory_space=pltpu.VMEM)],
        out_specs=pl.BlockSpec(memory_space=pltpu.VMEM),
        out_shape=jax.ShapeDtypeStruct((2, blocks, part, 256), BF),
        scratch_shapes=[
            pltpu.VMEM((blocks * part, 512), F32),
            pltpu.VMEM((256, 512), BF),
        ],
        compiler_params=pltpu.CompilerParams(vmem_limit_bytes=16 * 1024 * 1024),
        cost_estimate=pl.CostEstimate(
            flops=2 * blocks * part * 512 * sources * 128,
            bytes_accessed=2 * sources * height * 128 + 4 * blocks * part * 256,
            transcendentals=0,
        ),
    )(packed)


def local(hidden, weights, pattern, row_of_slot, cotangent):
    tokens = hidden.shape[0]
    half = tokens // 2
    owned, per_row, width = weights.shape[:3]
    flat = per_row * width
    shards = lax.axis_size("dp")
    me = lax.axis_index("blk")
    core = me % 2
    other = me + 1 - 2 * core
    first = core == 0

    def split(value):
        return jnp.transpose(value.reshape(half, owned, width), (1, 0, 2))

    with jax.named_scope("swap_tokens"):
        both = jnp.stack([hidden, cotangent])
        low, high = both[:, :half], both[:, half:]
        came = swap_cores(jnp.where(first, high, low))
        stays = jnp.where(first, low, high)
        mine, theirs = split(stays[0]), split(came[0])
        chip_blocks = jnp.where(
            first, jnp.concatenate([mine, theirs]), jnp.concatenate([theirs, mine])
        )
        grads = jnp.concatenate([split(stays[1]), split(came[1])])
    with jax.named_scope("gather_near"):
        near = near_exchange(jnp.broadcast_to(chip_blocks[None], (SIDE,) + chip_blocks.shape))
        near = near.reshape(SIDE * 2 * owned, half, width)
    with jax.named_scope("gather_far"):
        chunks = far_gather(near)
    with jax.named_scope("swap_weights"):
        ready, _ = lax.optimization_barrier((weights, near))
        other_weights = swap_cores(ready)
    with jax.named_scope("sources"):
        wanted = jnp.concatenate(
            [
                lax.dynamic_slice_in_dim(pattern, me * owned, owned, 0),
                lax.dynamic_slice_in_dim(pattern, other * owned, owned, 0),
            ]
        )
        slots = jnp.arange(row_of_slot.shape[0], dtype=jnp.int32)
        equal = row_of_slot[None, None, :] == wanted[:, :, None]
        source = jnp.sum(jnp.where(equal, slots[None, None, :], 0), axis=2)
        chip, inside = source // (2 * owned), source % (2 * owned)
        chip_y, chip_z = chip // SIDE, chip % SIDE
        my_y, my_z = me // (2 * SIDE), me // 2 % SIDE
        far = jnp.where(first, my_z, my_y)
        distance = (jnp.where(first, chip_z, chip_y) - far) * (1 - 2 * (far % 2)) % SIDE
        place = distance * SIDE + jnp.where(first, chip_y, chip_z)
        idx = (place * (2 * owned) + inside).reshape(-1)

    with jax.named_scope("blocks"):
        result, *terms, packed = run_blocks(
            core.reshape(1),
            idx,
            chunks,
            weights.reshape(owned, flat, 2 * width),
            other_weights.reshape(owned, flat, 2 * width),
            grads,
            shards,
        )

    def rejoin(keep, came):
        low = jnp.where(first, keep, came)
        high = jnp.where(first, came, keep)
        whole = jnp.stack([low, high])
        return jnp.transpose(whole, (0, 2, 1, 3)).reshape(tokens, owned * width)

    with jax.named_scope("reduce_far"):
        column = far_reduce(*terms)
    with jax.named_scope("weight_grad"):
        size = 2 * shards
        groups = [[i * size + j for j in range(size)] for i in range(DEVICES // 2)]
        packed = lax.all_to_all(packed, BOTH, 0, 0, axis_index_groups=groups, tiled=True)
        scale = 1.0 / math.sqrt(tokens * shards)
    with jax.named_scope("reduce_near"):
        column, packed = lax.optimization_barrier((column, packed))
        weight_grad = run_weights(packed, per_row, width // shards, scale)
        pieces = near_exchange(column.reshape(SIDE, 2 * owned * half, width))
        total = jnp.sum(pieces.astype(F32), axis=0).astype(BF)
        total, weight_grad = lax.optimization_barrier((total, weight_grad))
        total = total.reshape(2, owned, half, width)
    with jax.named_scope("swap_back"):
        keep = jnp.where(first, total[0], total[1])
        came = swap_cores(jnp.where(first, total[1], total[0]))
        input_grad = rejoin(keep, came)
        output = rejoin(result[:owned], swap_cores(result[owned:]))
    return (output, input_grad, weight_grad)


def solution(mesh):
    placed = (P("dp", "blk"), P("blk", None, None, None), P(), P(), P("dp", "blk"))
    return jax.shard_map(
        local,
        mesh=mesh,
        in_specs=placed,
        out_specs=(P("dp", "blk"), P("dp", "blk"), P("blk", None, "dp", None)),
        check_vma=False,
    )
```

```python
import math

import jax
import jax.numpy as jnp
from jax import lax
from jax.experimental import pallas as pl
from jax.experimental.pallas import tpu as pltpu
from jax.sharding import PartitionSpec as P

BF = jnp.bfloat16
F32 = jnp.float32
SIDE = 8
DEVICES = 2 * SIDE * SIDE
BOTH = ("blk", "dp")


def device_at(y, z, core):
    return (y % SIDE * SIDE + z % SIDE) * 2 + core


GROUPS_NEAR = [[device_at(y, z, 0) for y in range(SIDE)] for z in range(SIDE)] + [
    [device_at(y, z, 1) for z in range(SIDE)] for y in range(SIDE)
]
SWAP = [(i, i ^ 1) for i in range(DEVICES)]


def far_shift(value, by):
    pairs = []
    for y in range(SIDE):
        for z in range(SIDE):
            here = z + by * (1 - 2 * (z % 2))
            pairs.append((device_at(y, z, 0), device_at(y, here, 0)))
            here = y + by * (1 - 2 * (y % 2))
            pairs.append((device_at(y, z, 1), device_at(here, z, 1)))
    return lax.ppermute(value, "blk", pairs)


def swap_cores(value):
    return lax.ppermute(value, "blk", SWAP)


def near_exchange(value):
    return lax.all_to_all(value, "blk", 0, 0, axis_index_groups=GROUPS_NEAR, tiled=True)


def far_gather(own, beside):
    at6 = far_shift(own, 2)
    at2 = far_shift(own, -2)
    at1 = far_shift(own, 1)
    at6, beside = lax.optimization_barrier((at6, beside))
    at4 = far_shift(at6, 2)
    at3 = far_shift(at6, 1)
    at5 = far_shift(at2, -1)
    late, _, _ = lax.optimization_barrier((own, at2, at6))
    at7 = far_shift(late, -1)
    return (own, at1, at2, at3, at4, at5, at6, at7), beside


def far_reduce(own, to31, to57, to4, to2, to6):
    size = own.shape[0]
    got31 = far_shift(to31, 1)
    got57 = far_shift(to57, -1)
    got4 = far_shift(to4, 2)

    def add(*values):
        return sum(value.astype(F32) for value in values).astype(BF)

    sum6 = add(to6, got31[:size])
    to2, _ = lax.optimization_barrier((to2, sum6))
    sum2 = add(to2, got57[:size], got4)
    own, _ = lax.optimization_barrier((own, sum2))
    got6 = far_shift(sum6, -2)
    got2 = far_shift(sum2, 2)
    early = lax.optimization_barrier(
        own.astype(F32) + got31[size:].astype(F32) + got57[size:].astype(F32)
    )
    return add(early, got2, got6)


def block_kernel(core, idx, *refs):
    chunks = refs[:8]
    weights_here, weights_there, grads, out = refs[8:12]
    terms = refs[12:18]
    packed_out = refs[18]
    gathered, dense, kept, packed, weights, in_sems, out_sems, pack_sems, weight_sems = refs[19:]
    rows, tokens, wide = kept.shape
    flat = wide - 256
    blocks = flat // 128
    side = chunks[0].shape[0]

    def place(distance):
        return pl.ds(distance * side, side)

    loads = [
        pltpu.make_async_copy(ref, gathered.at[place(i)], in_sems.at[i])
        for i, ref in enumerate(chunks)
    ]
    weight_loads = [
        pltpu.make_async_copy(weights_here.at[i], weights.at[i], weight_sems.at[i])
        for i in range(rows // 2)
    ]
    for copy in loads + weight_loads:
        copy.start()
    dense[...] = jnp.zeros_like(dense)
    for copy in loads:
        copy.wait()
    for row in range(rows):
        for k in range(blocks):
            kept[row, :, k * 128 : (k + 1) * 128] = gathered[idx[row * blocks + k]]
    order = [2, 3, 0, 1]
    for row in order:
        if row < 2:
            weight_loads[row].wait()
        matrix = weights[row] if row < 2 else weights_there[row - 2]
        both = jnp.dot(kept[row, :, :flat], matrix, preferred_element_type=F32)
        gate = both[:, :128]
        upper = both[:, 128:]
        sigma = jax.nn.sigmoid(gate)
        out[row] = (gate * sigma * upper).astype(BF)
        gradf = grads[row].astype(F32)
        dgate = gradf * upper * sigma * (1.0 + gate * (1.0 - sigma))
        dup = gradf * gate * sigma
        kept[row, :, flat:] = jnp.concatenate([dgate, dup], axis=1).astype(BF)
    for row in order:
        matrix = weights[row] if row < 2 else weights_there[row - 2]
        partial = lax.dot_general(
            kept[row, :, flat:],
            matrix,
            (((1,), (1,)), ((), ())),
            preferred_element_type=F32,
        ).astype(BF)
        for start in range(0, blocks, 6):
            span = range(start, min(start + 6, blocks))
            values = [partial[:, k * 128 : (k + 1) * 128] for k in span]
            places_of = [idx[row * blocks + k] for k in span]
            if row < 2:
                values = [
                    (dense[at].astype(F32) + value.astype(F32)).astype(BF)
                    for at, value in zip(places_of, values)
                ]
            for at, value in zip(places_of, values):
                dense[at] = value
    own, to31, to57, to4, to2, to6 = terms
    pieces = [
        (to31.at[place(0)], place(3)),
        (to57.at[place(0)], place(5)),
        (to4, place(4)),
        (to31.at[place(1)], place(1)),
        (to57.at[place(1)], place(7)),
        (to2, place(2)),
        (to6, place(6)),
        (own, place(0)),
    ]
    stores = [
        pltpu.make_async_copy(dense.at[at], ref, out_sems.at[i])
        for i, (ref, at) in enumerate(pieces)
    ]
    for copy in stores:
        copy.start()
    shards = packed.shape[0] // 2
    part = 128 // shards
    for pair in range(2):
        base = lax.rem(core[0] + pair, 2) * shards
        for k in range(blocks):
            cut = slice(k * 128, (k + 1) * 128)
            turned = jnp.concatenate(
                [kept[2 * pair, :, cut], kept[2 * pair + 1, :, cut]], axis=0
            ).T
            for x in range(shards):
                packed[pair * shards + x, k * part : (k + 1) * part, :] = turned[
                    x * part : (x + 1) * part
                ]
        for row in range(2):
            for wing in range(2):
                value = kept[2 * pair + row, :, flat + wing * 128 : flat + (wing + 1) * 128]
                at = blocks * part + (2 * row + wing) * tokens
                for x in range(shards):
                    packed[pair * shards + x, at : at + tokens, :] = value
        copy = pltpu.make_async_copy(
            packed.at[pl.ds(pair * shards, shards)],
            packed_out.at[pl.ds(base, shards)],
            pack_sems.at[pair],
        )
        copy.start()
        stores.append(copy)
    for copy in stores:
        copy.wait()


def run_blocks(core, idx, chunks, weights, other_weights, grads, shards):
    rows, tokens = grads.shape[:2]
    flat = weights.shape[1]
    outside = pl.BlockSpec(memory_space=pl.ANY)
    whole = pl.BlockSpec(memory_space=pltpu.VMEM)
    scalars = pl.BlockSpec(memory_space=pltpu.SMEM)
    side = chunks[0].shape[0]
    total = SIDE * side
    lengths = (side, 2 * side, 2 * side, side, side, side)
    packed = (2 * shards, flat // shards + 4 * tokens, 128)
    return pl.pallas_call(
        block_kernel,
        in_specs=[scalars] * 2 + [outside] * 9 + [whole] * 2,
        out_specs=[whole] + [outside] * 7,
        out_shape=[jax.ShapeDtypeStruct((rows, tokens, 128), BF)]
        + [pltpu.HBM((n,) + chunks[0].shape[1:], BF) for n in lengths]
        + [pltpu.HBM(packed, BF)],
        scratch_shapes=[
            pltpu.VMEM((total, tokens, 128), BF),
            pltpu.VMEM((total, tokens, 128), BF),
            pltpu.VMEM((rows, tokens, flat + 256), BF),
            pltpu.VMEM(packed, BF),
            pltpu.VMEM(weights.shape, BF),
            pltpu.SemaphoreType.DMA((8,)),
            pltpu.SemaphoreType.DMA((8,)),
            pltpu.SemaphoreType.DMA((2,)),
            pltpu.SemaphoreType.DMA((2,)),
        ],
        compiler_params=pltpu.CompilerParams(vmem_limit_bytes=40 * 1024 * 1024),
        cost_estimate=pl.CostEstimate(
            flops=4 * rows * tokens * flat * 256,
            bytes_accessed=2 * rows * flat * 256 + 4 * total * tokens * 128,
            transcendentals=rows * tokens * 128,
        ),
    )(
        core,
        idx,
        *chunks,
        pltpu.with_memory_space_constraint(weights, pltpu.HBM),
        other_weights,
        grads,
    )


def weight_kernel(scale, packed, out, total, right):
    sources, height = packed.shape[:2]
    blocks, part = out.shape[1:3]
    flat = blocks * part
    tokens = (height - flat) // 4
    right[...] = jnp.zeros_like(right)
    for step in range(sources // 2):
        for i in range(2):
            for row in range(2):
                for side in range(2):
                    at = flat + (2 * row + side) * tokens
                    right[
                        (2 * i + row) * tokens : (2 * i + row + 1) * tokens,
                        row * 256 + side * 128 : row * 256 + (side + 1) * 128,
                    ] = packed[2 * step + i, at : at + tokens, :]
        left = jnp.concatenate([packed[2 * step, :flat, :], packed[2 * step + 1, :flat, :]], axis=1)
        product = jnp.dot(left, right[...], preferred_element_type=F32)
        if step == 0:
            total[...] = product
        else:
            total[...] += product
    for row in range(2):
        for k in range(blocks):
            value = total[k * part : (k + 1) * part, row * 256 : (row + 1) * 256]
            out[row, k] = (value * scale).astype(BF)


def run_weights(packed, blocks, part, scale):
    sources, height = packed.shape[:2]
    return pl.pallas_call(
        lambda *refs: weight_kernel(scale, *refs),
        in_specs=[pl.BlockSpec(memory_space=pltpu.VMEM)],
        out_specs=pl.BlockSpec(memory_space=pltpu.VMEM),
        out_shape=jax.ShapeDtypeStruct((2, blocks, part, 256), BF),
        scratch_shapes=[
            pltpu.VMEM((blocks * part, 512), F32),
            pltpu.VMEM((256, 512), BF),
        ],
        compiler_params=pltpu.CompilerParams(vmem_limit_bytes=16 * 1024 * 1024),
        cost_estimate=pl.CostEstimate(
            flops=2 * blocks * part * 512 * sources * 128,
            bytes_accessed=2 * sources * height * 128 + 4 * blocks * part * 256,
            transcendentals=0,
        ),
    )(packed)


def local(hidden, weights, pattern, row_of_slot, cotangent):
    tokens = hidden.shape[0]
    half = tokens // 2
    owned, per_row, width = weights.shape[:3]
    flat = per_row * width
    shards = lax.axis_size("dp")
    me = lax.axis_index("blk")
    core = me % 2
    other = me + 1 - 2 * core
    first = core == 0

    def split(value):
        return jnp.transpose(value.reshape(half, owned, width), (1, 0, 2))

    with jax.named_scope("swap_tokens"):
        both = jnp.stack([hidden, cotangent])
        low, high = both[:, :half], both[:, half:]
        came = swap_cores(jnp.where(first, high, low))
        stays = jnp.where(first, low, high)
        mine, theirs = split(stays[0]), split(came[0])
        chip_blocks = jnp.where(
            first, jnp.concatenate([mine, theirs]), jnp.concatenate([theirs, mine])
        )
        grads = jnp.concatenate([split(stays[1]), split(came[1])])
    with jax.named_scope("gather_near"):
        near = near_exchange(jnp.broadcast_to(chip_blocks[None], (SIDE,) + chip_blocks.shape))
        near = near.reshape(SIDE * 2 * owned, half, width)
    with jax.named_scope("gather_far"):
        ready, _ = lax.optimization_barrier((weights, near))
        chunks, other_weights = far_gather(near, swap_cores(ready))
    with jax.named_scope("sources"):
        wanted = jnp.concatenate(
            [
                lax.dynamic_slice_in_dim(pattern, me * owned, owned, 0),
                lax.dynamic_slice_in_dim(pattern, other * owned, owned, 0),
            ]
        )
        slots = jnp.arange(row_of_slot.shape[0], dtype=jnp.int32)
        equal = row_of_slot[None, None, :] == wanted[:, :, None]
        source = jnp.sum(jnp.where(equal, slots[None, None, :], 0), axis=2)
        chip, inside = source // (2 * owned), source % (2 * owned)
        chip_y, chip_z = chip // SIDE, chip % SIDE
        my_y, my_z = me // (2 * SIDE), me // 2 % SIDE
        far = jnp.where(first, my_z, my_y)
        distance = (jnp.where(first, chip_z, chip_y) - far) * (1 - 2 * (far % 2)) % SIDE
        place = distance * SIDE + jnp.where(first, chip_y, chip_z)
        idx = (place * (2 * owned) + inside).reshape(-1)

    with jax.named_scope("blocks"):
        result, *terms, packed = run_blocks(
            core.reshape(1),
            idx,
            chunks,
            weights.reshape(owned, flat, 2 * width),
            other_weights.reshape(owned, flat, 2 * width),
            grads,
            shards,
        )

    def rejoin(keep, came):
        low = jnp.where(first, keep, came)
        high = jnp.where(first, came, keep)
        whole = jnp.stack([low, high])
        return jnp.transpose(whole, (0, 2, 1, 3)).reshape(tokens, owned * width)

    with jax.named_scope("reduce_far"):
        column = far_reduce(*terms)
    with jax.named_scope("weight_grad"):
        size = 2 * shards
        groups = [[i * size + j for j in range(size)] for i in range(DEVICES // 2)]
        packed = lax.all_to_all(packed, BOTH, 0, 0, axis_index_groups=groups, tiled=True)
        scale = 1.0 / math.sqrt(tokens * shards)
    with jax.named_scope("reduce_near"):
        column, packed = lax.optimization_barrier((column, packed))
        weight_grad = run_weights(packed, per_row, width // shards, scale)
        pieces = near_exchange(column.reshape(SIDE, 2 * owned * half, width))
        total = jnp.sum(pieces.astype(F32), axis=0).astype(BF)
        total, weight_grad = lax.optimization_barrier((total, weight_grad))
        total = total.reshape(2, owned, half, width)
    with jax.named_scope("swap_back"):
        keep = jnp.where(first, total[0], total[1])
        came = swap_cores(jnp.where(first, total[1], total[0]))
        input_grad = rejoin(keep, came)
        output = rejoin(result[:owned], swap_cores(result[owned:]))
    return (output, input_grad, weight_grad)


def solution(mesh):
    placed = (P("dp", "blk"), P("blk", None, None, None), P(), P(), P("dp", "blk"))
    return jax.shard_map(
        local,
        mesh=mesh,
        in_specs=placed,
        out_specs=(P("dp", "blk"), P("dp", "blk"), P("blk", None, "dp", None)),
        check_vma=False,
    )
```

```python
import math

import jax
import jax.numpy as jnp
from jax import lax
from jax.experimental import pallas as pl
from jax.experimental.pallas import tpu as pltpu
from jax.sharding import PartitionSpec as P

BF = jnp.bfloat16
F32 = jnp.float32
SIDE = 8
DEVICES = 2 * SIDE * SIDE
BOTH = ("blk", "dp")


def device_at(y, z, core):
    return (y % SIDE * SIDE + z % SIDE) * 2 + core


GROUPS_NEAR = [[device_at(y, z, 0) for y in range(SIDE)] for z in range(SIDE)] + [
    [device_at(y, z, 1) for z in range(SIDE)] for y in range(SIDE)
]
SWAP = [(i, i ^ 1) for i in range(DEVICES)]


def far_shift(value, by):
    pairs = []
    for y in range(SIDE):
        for z in range(SIDE):
            here = z + by * (1 - 2 * (z % 2))
            pairs.append((device_at(y, z, 0), device_at(y, here, 0)))
            here = y + by * (1 - 2 * (y % 2))
            pairs.append((device_at(y, z, 1), device_at(here, z, 1)))
    return lax.ppermute(value, "blk", pairs)


def swap_cores(value):
    return lax.ppermute(value, "blk", SWAP)


def near_exchange(value):
    return lax.all_to_all(value, "blk", 0, 0, axis_index_groups=GROUPS_NEAR, tiled=True)


def far_gather(own, beside):
    at6 = far_shift(own, 2)
    at2 = far_shift(own, -2)
    at1 = far_shift(own, 1)
    at6, beside = lax.optimization_barrier((at6, beside))
    at4 = far_shift(at6, 2)
    at3 = far_shift(at6, 1)
    at5 = far_shift(at2, -1)
    late, _, _ = lax.optimization_barrier((own, at2, at6))
    at7 = far_shift(late, -1)
    return (own, at1, at2, at3, at4, at5, at6, at7), beside


def far_reduce(own, to31, to57, to4, to2, to6):
    size = own.shape[0]
    got31 = far_shift(to31, 1)
    got57 = far_shift(to57, -1)
    got4 = far_shift(to4, 2)

    def add(*values):
        return sum(value.astype(F32) for value in values).astype(BF)

    sum6 = add(to6, got31[:size])
    to2, _ = lax.optimization_barrier((to2, sum6))
    sum2 = add(to2, got57[:size], got4)
    own, _ = lax.optimization_barrier((own, sum2))
    got6 = far_shift(sum6, -2)
    got2 = far_shift(sum2, 2)
    early = lax.optimization_barrier(
        own.astype(F32) + got31[size:].astype(F32) + got57[size:].astype(F32)
    )
    return add(early, got2, got6)


def block_kernel(core, idx, *refs):
    chunks = refs[:8]
    weights_here, weights_there, grads, out = refs[8:12]
    terms = refs[12:18]
    packed_out = refs[18]
    gathered, dense, kept, packed, weights, in_sems, out_sems, pack_sems, weight_sems = refs[19:]
    rows, tokens, wide = kept.shape
    flat = wide - 256
    blocks = flat // 128
    side = chunks[0].shape[0]

    def place(distance):
        return pl.ds(distance * side, side)

    loads = [
        pltpu.make_async_copy(ref, gathered.at[place(i)], in_sems.at[i])
        for i, ref in enumerate(chunks)
    ]
    weight_loads = [
        pltpu.make_async_copy(weights_here.at[i], weights.at[i], weight_sems.at[i])
        for i in range(rows // 2)
    ]
    for copy in loads:
        copy.start()
    dense[...] = jnp.zeros_like(dense)
    for copy in loads:
        copy.wait()
    for copy in weight_loads:
        copy.start()
    for row in range(rows):
        for k in range(blocks):
            kept[row, :, k * 128 : (k + 1) * 128] = gathered[idx[row * blocks + k]]
    order = [2, 3, 0, 1]
    for row in order:
        if row < 2:
            weight_loads[row].wait()
        matrix = weights[row] if row < 2 else weights_there[row - 2]
        both = jnp.dot(kept[row, :, :flat], matrix, preferred_element_type=F32)
        gate = both[:, :128]
        upper = both[:, 128:]
        sigma = jax.nn.sigmoid(gate)
        out[row] = (gate * sigma * upper).astype(BF)
        gradf = grads[row].astype(F32)
        dgate = gradf * upper * sigma * (1.0 + gate * (1.0 - sigma))
        dup = gradf * gate * sigma
        kept[row, :, flat:] = jnp.concatenate([dgate, dup], axis=1).astype(BF)
    for row in order:
        matrix = weights[row] if row < 2 else weights_there[row - 2]
        partial = lax.dot_general(
            kept[row, :, flat:],
            matrix,
            (((1,), (1,)), ((), ())),
            preferred_element_type=F32,
        ).astype(BF)
        for start in range(0, blocks, 6):
            span = range(start, min(start + 6, blocks))
            values = [partial[:, k * 128 : (k + 1) * 128] for k in span]
            places_of = [idx[row * blocks + k] for k in span]
            if row < 2:
                values = [
                    (dense[at].astype(F32) + value.astype(F32)).astype(BF)
                    for at, value in zip(places_of, values)
                ]
            for at, value in zip(places_of, values):
                dense[at] = value
    own, to31, to57, to4, to2, to6 = terms
    pieces = [
        (to31.at[place(0)], place(3)),
        (to57.at[place(0)], place(5)),
        (to4, place(4)),
        (to31.at[place(1)], place(1)),
        (to57.at[place(1)], place(7)),
        (to2, place(2)),
        (to6, place(6)),
        (own, place(0)),
    ]
    stores = [
        pltpu.make_async_copy(dense.at[at], ref, out_sems.at[i])
        for i, (ref, at) in enumerate(pieces)
    ]
    for copy in stores:
        copy.start()
    shards = packed.shape[0] // 2
    part = 128 // shards
    for pair in range(2):
        base = lax.rem(core[0] + pair, 2) * shards
        for k in range(blocks):
            cut = slice(k * 128, (k + 1) * 128)
            turned = jnp.concatenate(
                [kept[2 * pair, :, cut], kept[2 * pair + 1, :, cut]], axis=0
            ).T
            for x in range(shards):
                packed[pair * shards + x, k * part : (k + 1) * part, :] = turned[
                    x * part : (x + 1) * part
                ]
        for row in range(2):
            for wing in range(2):
                value = kept[2 * pair + row, :, flat + wing * 128 : flat + (wing + 1) * 128]
                at = blocks * part + (2 * row + wing) * tokens
                for x in range(shards):
                    packed[pair * shards + x, at : at + tokens, :] = value
        copy = pltpu.make_async_copy(
            packed.at[pl.ds(pair * shards, shards)],
            packed_out.at[pl.ds(base, shards)],
            pack_sems.at[pair],
        )
        copy.start()
        stores.append(copy)
    for copy in stores:
        copy.wait()


def run_blocks(core, idx, chunks, weights, other_weights, grads, shards):
    rows, tokens = grads.shape[:2]
    flat = weights.shape[1]
    outside = pl.BlockSpec(memory_space=pl.ANY)
    whole = pl.BlockSpec(memory_space=pltpu.VMEM)
    scalars = pl.BlockSpec(memory_space=pltpu.SMEM)
    side = chunks[0].shape[0]
    total = SIDE * side
    lengths = (side, 2 * side, 2 * side, side, side, side)
    packed = (2 * shards, flat // shards + 4 * tokens, 128)
    return pl.pallas_call(
        block_kernel,
        in_specs=[scalars] * 2 + [outside] * 9 + [whole] * 2,
        out_specs=[whole] + [outside] * 7,
        out_shape=[jax.ShapeDtypeStruct((rows, tokens, 128), BF)]
        + [pltpu.HBM((n,) + chunks[0].shape[1:], BF) for n in lengths]
        + [pltpu.HBM(packed, BF)],
        scratch_shapes=[
            pltpu.VMEM((total, tokens, 128), BF),
            pltpu.VMEM((total, tokens, 128), BF),
            pltpu.VMEM((rows, tokens, flat + 256), BF),
            pltpu.VMEM(packed, BF),
            pltpu.VMEM(weights.shape, BF),
            pltpu.SemaphoreType.DMA((8,)),
            pltpu.SemaphoreType.DMA((8,)),
            pltpu.SemaphoreType.DMA((2,)),
            pltpu.SemaphoreType.DMA((2,)),
        ],
        compiler_params=pltpu.CompilerParams(vmem_limit_bytes=40 * 1024 * 1024),
        cost_estimate=pl.CostEstimate(
            flops=4 * rows * tokens * flat * 256,
            bytes_accessed=2 * rows * flat * 256 + 4 * total * tokens * 128,
            transcendentals=rows * tokens * 128,
        ),
    )(
        core,
        idx,
        *chunks,
        pltpu.with_memory_space_constraint(weights, pltpu.HBM),
        other_weights,
        grads,
    )


def weight_kernel(scale, packed, out, total, right):
    sources, height = packed.shape[:2]
    blocks, part = out.shape[1:3]
    flat = blocks * part
    tokens = (height - flat) // 4
    right[...] = jnp.zeros_like(right)
    for step in range(sources // 2):
        for i in range(2):
            for row in range(2):
                for side in range(2):
                    at = flat + (2 * row + side) * tokens
                    right[
                        (2 * i + row) * tokens : (2 * i + row + 1) * tokens,
                        row * 256 + side * 128 : row * 256 + (side + 1) * 128,
                    ] = packed[2 * step + i, at : at + tokens, :]
        left = jnp.concatenate([packed[2 * step, :flat, :], packed[2 * step + 1, :flat, :]], axis=1)
        product = jnp.dot(left, right[...], preferred_element_type=F32)
        if step == 0:
            total[...] = product
        else:
            total[...] += product
    for row in range(2):
        for k in range(blocks):
            value = total[k * part : (k + 1) * part, row * 256 : (row + 1) * 256]
            out[row, k] = (value * scale).astype(BF)


def run_weights(packed, blocks, part, scale):
    sources, height = packed.shape[:2]
    return pl.pallas_call(
        lambda *refs: weight_kernel(scale, *refs),
        in_specs=[pl.BlockSpec(memory_space=pltpu.VMEM)],
        out_specs=pl.BlockSpec(memory_space=pltpu.VMEM),
        out_shape=jax.ShapeDtypeStruct((2, blocks, part, 256), BF),
        scratch_shapes=[
            pltpu.VMEM((blocks * part, 512), F32),
            pltpu.VMEM((256, 512), BF),
        ],
        compiler_params=pltpu.CompilerParams(vmem_limit_bytes=16 * 1024 * 1024),
        cost_estimate=pl.CostEstimate(
            flops=2 * blocks * part * 512 * sources * 128,
            bytes_accessed=2 * sources * height * 128 + 4 * blocks * part * 256,
            transcendentals=0,
        ),
    )(packed)


def local(hidden, weights, pattern, row_of_slot, cotangent):
    tokens = hidden.shape[0]
    half = tokens // 2
    owned, per_row, width = weights.shape[:3]
    flat = per_row * width
    shards = lax.axis_size("dp")
    me = lax.axis_index("blk")
    core = me % 2
    other = me + 1 - 2 * core
    first = core == 0

    def split(value):
        return jnp.transpose(value.reshape(half, owned, width), (1, 0, 2))

    with jax.named_scope("swap_tokens"):
        both = jnp.stack([hidden, cotangent])
        low, high = both[:, :half], both[:, half:]
        came = swap_cores(jnp.where(first, high, low))
        stays = jnp.where(first, low, high)
        mine, theirs = split(stays[0]), split(came[0])
        chip_blocks = jnp.where(
            first, jnp.concatenate([mine, theirs]), jnp.concatenate([theirs, mine])
        )
        grads = jnp.concatenate([split(stays[1]), split(came[1])])
    with jax.named_scope("gather_near"):
        near = near_exchange(jnp.broadcast_to(chip_blocks[None], (SIDE,) + chip_blocks.shape))
        near = near.reshape(SIDE * 2 * owned, half, width)
    with jax.named_scope("gather_far"):
        ready, _ = lax.optimization_barrier((weights, near))
        chunks, other_weights = far_gather(near, swap_cores(ready))
    with jax.named_scope("sources"):
        wanted = jnp.concatenate(
            [
                lax.dynamic_slice_in_dim(pattern, me * owned, owned, 0),
                lax.dynamic_slice_in_dim(pattern, other * owned, owned, 0),
            ]
        )
        slots = jnp.arange(row_of_slot.shape[0], dtype=jnp.int32)
        equal = row_of_slot[None, None, :] == wanted[:, :, None]
        source = jnp.sum(jnp.where(equal, slots[None, None, :], 0), axis=2)
        chip, inside = source // (2 * owned), source % (2 * owned)
        chip_y, chip_z = chip // SIDE, chip % SIDE
        my_y, my_z = me // (2 * SIDE), me // 2 % SIDE
        far = jnp.where(first, my_z, my_y)
        distance = (jnp.where(first, chip_z, chip_y) - far) * (1 - 2 * (far % 2)) % SIDE
        place = distance * SIDE + jnp.where(first, chip_y, chip_z)
        idx = (place * (2 * owned) + inside).reshape(-1)

    with jax.named_scope("blocks"):
        result, *terms, packed = run_blocks(
            core.reshape(1),
            idx,
            chunks,
            weights.reshape(owned, flat, 2 * width),
            other_weights.reshape(owned, flat, 2 * width),
            grads,
            shards,
        )

    def rejoin(keep, came):
        low = jnp.where(first, keep, came)
        high = jnp.where(first, came, keep)
        return jnp.concatenate([jnp.concatenate(list(v), axis=1) for v in (low, high)])

    with jax.named_scope("reduce_far"):
        column = far_reduce(*terms)
    with jax.named_scope("weight_grad"):
        size = 2 * shards
        groups = [[i * size + j for j in range(size)] for i in range(DEVICES // 2)]
        packed = lax.all_to_all(packed, BOTH, 0, 0, axis_index_groups=groups, tiled=True)
        scale = 1.0 / math.sqrt(tokens * shards)
    with jax.named_scope("reduce_near"):
        column, packed = lax.optimization_barrier((column, packed))
        weight_grad = run_weights(packed, per_row, width // shards, scale)
        pieces = near_exchange(column.reshape(SIDE, 2 * owned * half, width))
        total = jnp.sum(pieces.astype(F32), axis=0).astype(BF)
        total, weight_grad = lax.optimization_barrier((total, weight_grad))
        total = total.reshape(2, owned, half, width)
    with jax.named_scope("swap_back"):
        keep = jnp.where(first, total[0], total[1])
        came = swap_cores(jnp.where(first, total[1], total[0]))
        input_grad = rejoin(keep, came)
        output = rejoin(result[:owned], swap_cores(result[owned:]))
    return (output, input_grad, weight_grad)


def solution(mesh):
    placed = (P("dp", "blk"), P("blk", None, None, None), P(), P(), P("dp", "blk"))
    return jax.shard_map(
        local,
        mesh=mesh,
        in_specs=placed,
        out_specs=(P("dp", "blk"), P("dp", "blk"), P("blk", None, "dp", None)),
        check_vma=False,
    )
```

```python
import math

import jax
import jax.numpy as jnp
from jax import lax
from jax.experimental import pallas as pl
from jax.experimental.pallas import tpu as pltpu
from jax.sharding import PartitionSpec as P

BF = jnp.bfloat16
F32 = jnp.float32
SIDE = 8
DEVICES = 2 * SIDE * SIDE
BOTH = ("blk", "dp")


def device_at(y, z, core):
    return (y % SIDE * SIDE + z % SIDE) * 2 + core


GROUPS_NEAR = [[device_at(y, z, 0) for y in range(SIDE)] for z in range(SIDE)] + [
    [device_at(y, z, 1) for z in range(SIDE)] for y in range(SIDE)
]
SWAP = [(i, i ^ 1) for i in range(DEVICES)]


def far_shift(value, by):
    pairs = []
    for y in range(SIDE):
        for z in range(SIDE):
            here = z + by * (1 - 2 * (z % 2))
            pairs.append((device_at(y, z, 0), device_at(y, here, 0)))
            here = y + by * (1 - 2 * (y % 2))
            pairs.append((device_at(y, z, 1), device_at(here, z, 1)))
    return lax.ppermute(value, "blk", pairs)


def swap_cores(value):
    return lax.ppermute(value, "blk", SWAP)


def near_exchange(value):
    return lax.all_to_all(value, "blk", 0, 0, axis_index_groups=GROUPS_NEAR, tiled=True)


def far_gather(own, beside):
    at6 = far_shift(own, 2)
    at2 = far_shift(own, -2)
    at1 = far_shift(own, 1)
    at6, beside = lax.optimization_barrier((at6, beside))
    at4 = far_shift(at6, 2)
    at3 = far_shift(at6, 1)
    at5 = far_shift(at2, -1)
    late, _, _ = lax.optimization_barrier((own, at2, at6))
    at7 = far_shift(late, -1)
    return (own, at1, at2, at3, at4, at5, at6, at7), beside


def far_reduce(own, to31, to57, to4, to2, to6):
    size = own.shape[0]
    got31 = far_shift(to31, 1)
    got57 = far_shift(to57, -1)
    got4 = far_shift(to4, 2)

    def add(*values):
        return sum(value.astype(F32) for value in values).astype(BF)

    sum6 = add(to6, got31[:size])
    to2, _ = lax.optimization_barrier((to2, sum6))
    sum2 = add(to2, got57[:size], got4)
    own, _ = lax.optimization_barrier((own, sum2))
    got6 = far_shift(sum6, -2)
    got2 = far_shift(sum2, 2)
    early = lax.optimization_barrier(
        own.astype(F32) + got31[size:].astype(F32) + got57[size:].astype(F32)
    )
    return add(early, got2, got6)


def block_kernel(core, idx, *refs):
    chunks = refs[:8]
    weights_here, weights_there, grads, out = refs[8:12]
    terms = refs[12:18]
    packed_out = refs[18]
    gathered, dense, kept, packed, weights, in_sems, out_sems, pack_sems, weight_sems = refs[19:]
    rows, tokens, wide = kept.shape
    flat = wide - 256
    blocks = flat // 128
    side = chunks[0].shape[0]

    def place(distance):
        return pl.ds(distance * side, side)

    loads = [
        pltpu.make_async_copy(ref, gathered.at[place(i)], in_sems.at[i])
        for i, ref in enumerate(chunks)
    ]
    weight_loads = [
        pltpu.make_async_copy(weights_here.at[i], weights.at[i], weight_sems.at[i])
        for i in range(rows // 2)
    ]
    for copy in loads + weight_loads:
        copy.start()
    dense[...] = jnp.zeros_like(dense)
    for copy in loads:
        copy.wait()
    for row in range(rows):
        for k in range(blocks):
            kept[row, :, k * 128 : (k + 1) * 128] = gathered[idx[row * blocks + k]]
    order = [2, 3, 0, 1]
    for row in order:
        if row < 2:
            weight_loads[row].wait()
        matrix = weights[row] if row < 2 else weights_there[row - 2]
        both = jnp.dot(kept[row, :, :flat], matrix, preferred_element_type=F32)
        gate = both[:, :128]
        upper = both[:, 128:]
        sigma = jax.nn.sigmoid(gate)
        out[row] = (gate * sigma * upper).astype(BF)
        gradf = grads[row].astype(F32)
        dgate = gradf * upper * sigma * (1.0 + gate * (1.0 - sigma))
        dup = gradf * gate * sigma
        kept[row, :, flat:] = jnp.concatenate([dgate, dup], axis=1).astype(BF)
    for row in order:
        matrix = weights[row] if row < 2 else weights_there[row - 2]
        partial = lax.dot_general(
            kept[row, :, flat:],
            matrix,
            (((1,), (1,)), ((), ())),
            preferred_element_type=F32,
        ).astype(BF)
        for start in range(0, blocks, 6):
            span = range(start, min(start + 6, blocks))
            values = [partial[:, k * 128 : (k + 1) * 128] for k in span]
            places_of = [idx[row * blocks + k] for k in span]
            if row < 2:
                values = [
                    (dense[at].astype(F32) + value.astype(F32)).astype(BF)
                    for at, value in zip(places_of, values)
                ]
            for at, value in zip(places_of, values):
                dense[at] = value
    own, to31, to57, to4, to2, to6 = terms
    pieces = [
        (to31.at[place(0)], place(3)),
        (to57.at[place(0)], place(5)),
        (to4, place(4)),
        (to31.at[place(1)], place(1)),
        (to57.at[place(1)], place(7)),
        (to2, place(2)),
        (to6, place(6)),
        (own, place(0)),
    ]
    stores = [
        pltpu.make_async_copy(dense.at[at], ref, out_sems.at[i])
        for i, (ref, at) in enumerate(pieces)
    ]
    for copy in stores:
        copy.start()
    shards = packed.shape[0] // 2
    part = 128 // shards
    for pair in range(2):
        base = lax.rem(core[0] + pair, 2) * shards
        for k in range(blocks):
            cut = slice(k * 128, (k + 1) * 128)
            turned = jnp.concatenate(
                [kept[2 * pair, :, cut], kept[2 * pair + 1, :, cut]], axis=0
            ).T
            for x in range(shards):
                packed[pair * shards + x, k * part : (k + 1) * part, :] = turned[
                    x * part : (x + 1) * part
                ]
        for row in range(2):
            for wing in range(2):
                value = kept[2 * pair + row, :, flat + wing * 128 : flat + (wing + 1) * 128]
                at = blocks * part + (2 * row + wing) * tokens
                for x in range(shards):
                    packed[pair * shards + x, at : at + tokens, :] = value
        copy = pltpu.make_async_copy(
            packed.at[pl.ds(pair * shards, shards)],
            packed_out.at[pl.ds(base, shards)],
            pack_sems.at[pair],
        )
        copy.start()
        stores.append(copy)
    for copy in stores:
        copy.wait()


def run_blocks(core, idx, chunks, weights, other_weights, grads, shards):
    rows, tokens = grads.shape[:2]
    flat = weights.shape[1]
    outside = pl.BlockSpec(memory_space=pl.ANY)
    whole = pl.BlockSpec(memory_space=pltpu.VMEM)
    scalars = pl.BlockSpec(memory_space=pltpu.SMEM)
    side = chunks[0].shape[0]
    total = SIDE * side
    lengths = (side, 2 * side, 2 * side, side, side, side)
    packed = (2 * shards, flat // shards + 4 * tokens, 128)
    return pl.pallas_call(
        block_kernel,
        in_specs=[scalars] * 2 + [outside] * 9 + [whole] * 2,
        out_specs=[whole] + [outside] * 7,
        out_shape=[jax.ShapeDtypeStruct((rows, tokens, 128), BF)]
        + [pltpu.HBM((n,) + chunks[0].shape[1:], BF) for n in lengths]
        + [pltpu.HBM(packed, BF)],
        scratch_shapes=[
            pltpu.VMEM((total, tokens, 128), BF),
            pltpu.VMEM((total, tokens, 128), BF),
            pltpu.VMEM((rows, tokens, flat + 256), BF),
            pltpu.VMEM(packed, BF),
            pltpu.VMEM(weights.shape, BF),
            pltpu.SemaphoreType.DMA((8,)),
            pltpu.SemaphoreType.DMA((8,)),
            pltpu.SemaphoreType.DMA((2,)),
            pltpu.SemaphoreType.DMA((2,)),
        ],
        compiler_params=pltpu.CompilerParams(vmem_limit_bytes=40 * 1024 * 1024),
        cost_estimate=pl.CostEstimate(
            flops=4 * rows * tokens * flat * 256,
            bytes_accessed=2 * rows * flat * 256 + 4 * total * tokens * 128,
            transcendentals=rows * tokens * 128,
        ),
    )(
        core,
        idx,
        *chunks,
        pltpu.with_memory_space_constraint(weights, pltpu.HBM),
        other_weights,
        grads,
    )


def weight_kernel(scale, packed, out, total, right):
    sources, height = packed.shape[:2]
    blocks, part = out.shape[1:3]
    flat = blocks * part
    tokens = (height - flat) // 4
    right[...] = jnp.zeros_like(right)
    for step in range(sources // 2):
        for i in range(2):
            for row in range(2):
                for side in range(2):
                    at = flat + (2 * row + side) * tokens
                    right[
                        (2 * i + row) * tokens : (2 * i + row + 1) * tokens,
                        row * 256 + side * 128 : row * 256 + (side + 1) * 128,
                    ] = packed[2 * step + i, at : at + tokens, :]
        left = jnp.concatenate([packed[2 * step, :flat, :], packed[2 * step + 1, :flat, :]], axis=1)
        product = jnp.dot(left, right[...], preferred_element_type=F32)
        if step == 0:
            total[...] = product
        else:
            total[...] += product
    for row in range(2):
        for k in range(blocks):
            value = total[k * part : (k + 1) * part, row * 256 : (row + 1) * 256]
            out[row, k] = (value * scale).astype(BF)


def run_weights(packed, blocks, part, scale):
    sources, height = packed.shape[:2]
    return pl.pallas_call(
        lambda *refs: weight_kernel(scale, *refs),
        in_specs=[pl.BlockSpec(memory_space=pltpu.VMEM)],
        out_specs=pl.BlockSpec(memory_space=pltpu.VMEM),
        out_shape=jax.ShapeDtypeStruct((2, blocks, part, 256), BF),
        scratch_shapes=[
            pltpu.VMEM((blocks * part, 512), F32),
            pltpu.VMEM((256, 512), BF),
        ],
        compiler_params=pltpu.CompilerParams(vmem_limit_bytes=16 * 1024 * 1024),
        cost_estimate=pl.CostEstimate(
            flops=2 * blocks * part * 512 * sources * 128,
            bytes_accessed=2 * sources * height * 128 + 4 * blocks * part * 256,
            transcendentals=0,
        ),
    )(packed)


def local(hidden, weights, pattern, row_of_slot, cotangent):
    tokens = hidden.shape[0]
    half = tokens // 2
    owned, per_row, width = weights.shape[:3]
    flat = per_row * width
    shards = lax.axis_size("dp")
    me = lax.axis_index("blk")
    core = me % 2
    other = me + 1 - 2 * core
    first = core == 0

    def split(value):
        return jnp.transpose(value.reshape(half, owned, width), (1, 0, 2))

    with jax.named_scope("swap_tokens"):
        both = jnp.stack([hidden, cotangent])
        low, high = both[:, :half], both[:, half:]
        came = swap_cores(jnp.where(first, high, low))
        stays = jnp.where(first, low, high)
        mine, theirs = split(stays[0]), split(came[0])
        chip_blocks = jnp.where(
            first, jnp.concatenate([mine, theirs]), jnp.concatenate([theirs, mine])
        )
        grads = jnp.concatenate([split(stays[1]), split(came[1])])
    with jax.named_scope("gather_near"):
        near = near_exchange(jnp.broadcast_to(chip_blocks[None], (SIDE,) + chip_blocks.shape))
        near = near.reshape(SIDE * 2 * owned, half, width)
    with jax.named_scope("gather_far"):
        ready, _ = lax.optimization_barrier((weights, near))
        chunks, other_weights = far_gather(near, swap_cores(ready))
    with jax.named_scope("sources"):
        wanted = jnp.concatenate(
            [
                lax.dynamic_slice_in_dim(pattern, me * owned, owned, 0),
                lax.dynamic_slice_in_dim(pattern, other * owned, owned, 0),
            ]
        )
        slots = jnp.arange(row_of_slot.shape[0], dtype=jnp.int32)
        equal = row_of_slot[None, None, :] == wanted[:, :, None]
        source = jnp.sum(jnp.where(equal, slots[None, None, :], 0), axis=2)
        chip, inside = source // (2 * owned), source % (2 * owned)
        chip_y, chip_z = chip // SIDE, chip % SIDE
        my_y, my_z = me // (2 * SIDE), me // 2 % SIDE
        far = jnp.where(first, my_z, my_y)
        distance = (jnp.where(first, chip_z, chip_y) - far) * (1 - 2 * (far % 2)) % SIDE
        place = distance * SIDE + jnp.where(first, chip_y, chip_z)
        idx = (place * (2 * owned) + inside).reshape(-1)

    with jax.named_scope("blocks"):
        result, *terms, packed = run_blocks(
            core.reshape(1),
            idx,
            chunks,
            weights.reshape(owned, flat, 2 * width),
            other_weights.reshape(owned, flat, 2 * width),
            grads,
            shards,
        )

    def rejoin(keep, came):
        low = jnp.where(first, keep, came)
        high = jnp.where(first, came, keep)
        return jnp.concatenate([jnp.concatenate(list(v), axis=1) for v in (low, high)])

    with jax.named_scope("reduce_far"):
        column = far_reduce(*terms)
    with jax.named_scope("weight_grad"):
        size = 2 * shards
        groups = [[i * size + j for j in range(size)] for i in range(DEVICES // 2)]
        packed = lax.all_to_all(packed, BOTH, 0, 0, axis_index_groups=groups, tiled=True)
        scale = 1.0 / math.sqrt(tokens * shards)
    with jax.named_scope("reduce_near"):
        column, packed = lax.optimization_barrier((column, packed))
        weight_grad = run_weights(packed, per_row, width // shards, scale)
        pieces = near_exchange(column.reshape(SIDE, 2 * owned * half, width))
        total = jnp.sum(pieces.astype(F32), axis=0).astype(BF)
        total, weight_grad = lax.optimization_barrier((total, weight_grad))
        total = total.reshape(2, owned, half, width)
    with jax.named_scope("swap_back"):
        keep = jnp.where(first, total[0], total[1])
        came = swap_cores(jnp.where(first, total[1], total[0]))
        input_grad = rejoin(keep, came)
        output = rejoin(result[:owned], swap_cores(result[owned:]))
    return (output, input_grad, weight_grad)


def solution(mesh):
    placed = (P("dp", "blk"), P("blk", None, None, None), P(), P(), P("dp", "blk"))
    return jax.shard_map(
        local,
        mesh=mesh,
        in_specs=placed,
        out_specs=(P("dp", "blk"), P("dp", "blk"), P("blk", None, "dp", None)),
        check_vma=False,
    )
```

```python
import math

import jax
import jax.numpy as jnp
from jax import lax
from jax.experimental import pallas as pl
from jax.experimental.pallas import tpu as pltpu
from jax.sharding import PartitionSpec as P

BF = jnp.bfloat16
F32 = jnp.float32
SIDE = 8
DEVICES = 2 * SIDE * SIDE
BOTH = ("blk", "dp")


def device_at(y, z, core):
    return (y % SIDE * SIDE + z % SIDE) * 2 + core


GROUPS_NEAR = [[device_at(y, z, 0) for y in range(SIDE)] for z in range(SIDE)] + [
    [device_at(y, z, 1) for z in range(SIDE)] for y in range(SIDE)
]
SWAP = [(i, i ^ 1) for i in range(DEVICES)]


def far_shift(value, by):
    pairs = []
    for y in range(SIDE):
        for z in range(SIDE):
            here = z + by * (1 - 2 * (z % 2))
            pairs.append((device_at(y, z, 0), device_at(y, here, 0)))
            here = y + by * (1 - 2 * (y % 2))
            pairs.append((device_at(y, z, 1), device_at(here, z, 1)))
    return lax.ppermute(value, "blk", pairs)


def swap_cores(value):
    return lax.ppermute(value, "blk", SWAP)


def near_exchange(value):
    return lax.all_to_all(value, "blk", 0, 0, axis_index_groups=GROUPS_NEAR, tiled=True)


def far_gather(own, beside):
    at6 = far_shift(own, 2)
    at2 = far_shift(own, -2)
    at1 = far_shift(own, 1)
    at6, beside = lax.optimization_barrier((at6, beside))
    at4 = far_shift(at6, 2)
    at3 = far_shift(at6, 1)
    at5 = far_shift(at2, -1)
    late, _, _ = lax.optimization_barrier((own, at2, at6))
    at7 = far_shift(late, -1)
    return (own, at1, at2, at3, at4, at5, at6, at7), beside


def far_reduce(own, to31, to57, to4, to2, to6):
    size = own.shape[0]
    got31 = far_shift(to31, 1)
    got57 = far_shift(to57, -1)
    got4 = far_shift(to4, 2)

    def add(*values):
        return sum(value.astype(F32) for value in values).astype(BF)

    sum6 = add(to6, got31[:size])
    to2, _ = lax.optimization_barrier((to2, sum6))
    sum2 = add(to2, got57[:size], got4)
    own, _ = lax.optimization_barrier((own, sum2))
    got6 = far_shift(sum6, -2)
    got2 = far_shift(sum2, 2)
    early = lax.optimization_barrier(
        own.astype(F32) + got31[size:].astype(F32) + got57[size:].astype(F32)
    )
    return add(early, got2, got6)


def block_kernel(core, idx, *refs):
    chunks = refs[:8]
    weights_here, weights_there, grads, out = refs[8:12]
    terms = refs[12:18]
    packed_out = refs[18]
    gathered, dense, kept, packed, weights, in_sems, out_sems, pack_sems, weight_sems = refs[19:]
    rows, tokens, wide = kept.shape
    flat = wide - 256
    blocks = flat // 128
    side = chunks[0].shape[0]

    def place(distance):
        return pl.ds(distance * side, side)

    loads = [
        pltpu.make_async_copy(ref, gathered.at[place(i)], in_sems.at[i])
        for i, ref in enumerate(chunks)
    ]
    weight_loads = [
        pltpu.make_async_copy(weights_here.at[i], weights.at[i], weight_sems.at[i])
        for i in range(rows // 2)
    ]
    for copy in loads:
        copy.start()
    for copy in weight_loads:
        copy.start(priority=1)
    dense[...] = jnp.zeros_like(dense)
    for copy in loads:
        copy.wait()
    for row in range(rows):
        for k in range(blocks):
            kept[row, :, k * 128 : (k + 1) * 128] = gathered[idx[row * blocks + k]]
    order = [2, 3, 0, 1]
    for row in order:
        if row < 2:
            weight_loads[row].wait()
        matrix = weights[row] if row < 2 else weights_there[row - 2]
        both = jnp.dot(kept[row, :, :flat], matrix, preferred_element_type=F32)
        gate = both[:, :128]
        upper = both[:, 128:]
        sigma = jax.nn.sigmoid(gate)
        out[row] = (gate * sigma * upper).astype(BF)
        gradf = grads[row].astype(F32)
        dgate = gradf * upper * sigma * (1.0 + gate * (1.0 - sigma))
        dup = gradf * gate * sigma
        kept[row, :, flat:] = jnp.concatenate([dgate, dup], axis=1).astype(BF)
    for row in order:
        matrix = weights[row] if row < 2 else weights_there[row - 2]
        partial = lax.dot_general(
            kept[row, :, flat:],
            matrix,
            (((1,), (1,)), ((), ())),
            preferred_element_type=F32,
        ).astype(BF)
        for start in range(0, blocks, 6):
            span = range(start, min(start + 6, blocks))
            values = [partial[:, k * 128 : (k + 1) * 128] for k in span]
            places_of = [idx[row * blocks + k] for k in span]
            if row < 2:
                values = [
                    (dense[at].astype(F32) + value.astype(F32)).astype(BF)
                    for at, value in zip(places_of, values)
                ]
            for at, value in zip(places_of, values):
                dense[at] = value
    own, to31, to57, to4, to2, to6 = terms
    pieces = [
        (to31.at[place(0)], place(3)),
        (to57.at[place(0)], place(5)),
        (to4, place(4)),
        (to31.at[place(1)], place(1)),
        (to57.at[place(1)], place(7)),
        (to2, place(2)),
        (to6, place(6)),
        (own, place(0)),
    ]
    stores = [
        pltpu.make_async_copy(dense.at[at], ref, out_sems.at[i])
        for i, (ref, at) in enumerate(pieces)
    ]
    for copy in stores:
        copy.start()
    shards = packed.shape[0] // 2
    part = 128 // shards
    for pair in range(2):
        base = lax.rem(core[0] + pair, 2) * shards
        for k in range(blocks):
            cut = slice(k * 128, (k + 1) * 128)
            turned = jnp.concatenate(
                [kept[2 * pair, :, cut], kept[2 * pair + 1, :, cut]], axis=0
            ).T
            for x in range(shards):
                packed[pair * shards + x, k * part : (k + 1) * part, :] = turned[
                    x * part : (x + 1) * part
                ]
        for row in range(2):
            for wing in range(2):
                value = kept[2 * pair + row, :, flat + wing * 128 : flat + (wing + 1) * 128]
                at = blocks * part + (2 * row + wing) * tokens
                for x in range(shards):
                    packed[pair * shards + x, at : at + tokens, :] = value
        copy = pltpu.make_async_copy(
            packed.at[pl.ds(pair * shards, shards)],
            packed_out.at[pl.ds(base, shards)],
            pack_sems.at[pair],
        )
        copy.start()
        stores.append(copy)
    for copy in stores:
        copy.wait()


def run_blocks(core, idx, chunks, weights, other_weights, grads, shards):
    rows, tokens = grads.shape[:2]
    flat = weights.shape[1]
    outside = pl.BlockSpec(memory_space=pl.ANY)
    whole = pl.BlockSpec(memory_space=pltpu.VMEM)
    scalars = pl.BlockSpec(memory_space=pltpu.SMEM)
    side = chunks[0].shape[0]
    total = SIDE * side
    lengths = (side, 2 * side, 2 * side, side, side, side)
    packed = (2 * shards, flat // shards + 4 * tokens, 128)
    return pl.pallas_call(
        block_kernel,
        in_specs=[scalars] * 2 + [outside] * 9 + [whole] * 2,
        out_specs=[whole] + [outside] * 7,
        out_shape=[jax.ShapeDtypeStruct((rows, tokens, 128), BF)]
        + [pltpu.HBM((n,) + chunks[0].shape[1:], BF) for n in lengths]
        + [pltpu.HBM(packed, BF)],
        scratch_shapes=[
            pltpu.VMEM((total, tokens, 128), BF),
            pltpu.VMEM((total, tokens, 128), BF),
            pltpu.VMEM((rows, tokens, flat + 256), BF),
            pltpu.VMEM(packed, BF),
            pltpu.VMEM(weights.shape, BF),
            pltpu.SemaphoreType.DMA((8,)),
            pltpu.SemaphoreType.DMA((8,)),
            pltpu.SemaphoreType.DMA((2,)),
            pltpu.SemaphoreType.DMA((2,)),
        ],
        compiler_params=pltpu.CompilerParams(vmem_limit_bytes=40 * 1024 * 1024),
        cost_estimate=pl.CostEstimate(
            flops=4 * rows * tokens * flat * 256,
            bytes_accessed=2 * rows * flat * 256 + 4 * total * tokens * 128,
            transcendentals=rows * tokens * 128,
        ),
    )(
        core,
        idx,
        *chunks,
        pltpu.with_memory_space_constraint(weights, pltpu.HBM),
        other_weights,
        grads,
    )


def weight_kernel(scale, packed, out, total, right):
    sources, height = packed.shape[:2]
    blocks, part = out.shape[1:3]
    flat = blocks * part
    tokens = (height - flat) // 4
    right[...] = jnp.zeros_like(right)
    for step in range(sources // 2):
        for i in range(2):
            for row in range(2):
                for side in range(2):
                    at = flat + (2 * row + side) * tokens
                    right[
                        (2 * i + row) * tokens : (2 * i + row + 1) * tokens,
                        row * 256 + side * 128 : row * 256 + (side + 1) * 128,
                    ] = packed[2 * step + i, at : at + tokens, :]
        left = jnp.concatenate([packed[2 * step, :flat, :], packed[2 * step + 1, :flat, :]], axis=1)
        product = jnp.dot(left, right[...], preferred_element_type=F32)
        if step == 0:
            total[...] = product
        else:
            total[...] += product
    for row in range(2):
        for k in range(blocks):
            value = total[k * part : (k + 1) * part, row * 256 : (row + 1) * 256]
            out[row, k] = (value * scale).astype(BF)


def run_weights(packed, blocks, part, scale):
    sources, height = packed.shape[:2]
    return pl.pallas_call(
        lambda *refs: weight_kernel(scale, *refs),
        in_specs=[pl.BlockSpec(memory_space=pltpu.VMEM)],
        out_specs=pl.BlockSpec(memory_space=pltpu.VMEM),
        out_shape=jax.ShapeDtypeStruct((2, blocks, part, 256), BF),
        scratch_shapes=[
            pltpu.VMEM((blocks * part, 512), F32),
            pltpu.VMEM((256, 512), BF),
        ],
        compiler_params=pltpu.CompilerParams(vmem_limit_bytes=16 * 1024 * 1024),
        cost_estimate=pl.CostEstimate(
            flops=2 * blocks * part * 512 * sources * 128,
            bytes_accessed=2 * sources * height * 128 + 4 * blocks * part * 256,
            transcendentals=0,
        ),
    )(packed)


def local(hidden, weights, pattern, row_of_slot, cotangent):
    tokens = hidden.shape[0]
    half = tokens // 2
    owned, per_row, width = weights.shape[:3]
    flat = per_row * width
    shards = lax.axis_size("dp")
    me = lax.axis_index("blk")
    core = me % 2
    other = me + 1 - 2 * core
    first = core == 0

    def split(value):
        return jnp.transpose(value.reshape(half, owned, width), (1, 0, 2))

    with jax.named_scope("swap_tokens"):
        both = jnp.stack([hidden, cotangent])
        low, high = both[:, :half], both[:, half:]
        came = swap_cores(jnp.where(first, high, low))
        stays = jnp.where(first, low, high)
        mine, theirs = split(stays[0]), split(came[0])
        chip_blocks = jnp.where(
            first, jnp.concatenate([mine, theirs]), jnp.concatenate([theirs, mine])
        )
        grads = jnp.concatenate([split(stays[1]), split(came[1])])
    with jax.named_scope("gather_near"):
        near = near_exchange(jnp.broadcast_to(chip_blocks[None], (SIDE,) + chip_blocks.shape))
        near = near.reshape(SIDE * 2 * owned, half, width)
    with jax.named_scope("gather_far"):
        ready, _ = lax.optimization_barrier((weights, near))
        chunks, other_weights = far_gather(near, swap_cores(ready))
    with jax.named_scope("sources"):
        wanted = jnp.concatenate(
            [
                lax.dynamic_slice_in_dim(pattern, me * owned, owned, 0),
                lax.dynamic_slice_in_dim(pattern, other * owned, owned, 0),
            ]
        )
        slots = jnp.arange(row_of_slot.shape[0], dtype=jnp.int32)
        equal = row_of_slot[None, None, :] == wanted[:, :, None]
        source = jnp.sum(jnp.where(equal, slots[None, None, :], 0), axis=2)
        chip, inside = source // (2 * owned), source % (2 * owned)
        chip_y, chip_z = chip // SIDE, chip % SIDE
        my_y, my_z = me // (2 * SIDE), me // 2 % SIDE
        far = jnp.where(first, my_z, my_y)
        distance = (jnp.where(first, chip_z, chip_y) - far) * (1 - 2 * (far % 2)) % SIDE
        place = distance * SIDE + jnp.where(first, chip_y, chip_z)
        idx = (place * (2 * owned) + inside).reshape(-1)

    with jax.named_scope("blocks"):
        result, *terms, packed = run_blocks(
            core.reshape(1),
            idx,
            chunks,
            weights.reshape(owned, flat, 2 * width),
            other_weights.reshape(owned, flat, 2 * width),
            grads,
            shards,
        )

    def rejoin(keep, came):
        low = jnp.where(first, keep, came)
        high = jnp.where(first, came, keep)
        whole = jnp.stack([low, high])
        return jnp.transpose(whole, (0, 2, 1, 3)).reshape(tokens, owned * width)

    with jax.named_scope("reduce_far"):
        column = far_reduce(*terms)
    with jax.named_scope("weight_grad"):
        size = 2 * shards
        groups = [[i * size + j for j in range(size)] for i in range(DEVICES // 2)]
        packed = lax.all_to_all(packed, BOTH, 0, 0, axis_index_groups=groups, tiled=True)
        scale = 1.0 / math.sqrt(tokens * shards)
    with jax.named_scope("reduce_near"):
        column, packed = lax.optimization_barrier((column, packed))
        weight_grad = run_weights(packed, per_row, width // shards, scale)
        pieces = near_exchange(column.reshape(SIDE, 2 * owned * half, width))
        total = jnp.sum(pieces.astype(F32), axis=0).astype(BF)
        total, weight_grad = lax.optimization_barrier((total, weight_grad))
        total = total.reshape(2, owned, half, width)
    with jax.named_scope("swap_back"):
        keep = jnp.where(first, total[0], total[1])
        came = swap_cores(jnp.where(first, total[1], total[0]))
        input_grad = rejoin(keep, came)
        output = rejoin(result[:owned], swap_cores(result[owned:]))
    return (output, input_grad, weight_grad)


def solution(mesh):
    placed = (P("dp", "blk"), P("blk", None, None, None), P(), P(), P("dp", "blk"))
    return jax.shard_map(
        local,
        mesh=mesh,
        in_specs=placed,
        out_specs=(P("dp", "blk"), P("dp", "blk"), P("blk", None, "dp", None)),
        check_vma=False,
    )
```
